32 devices in a mesh: row: 4 (over z), col: 8 (over y, x, core).
Axes of the slice: x: 2, y: 2, z: 4, core: 2. Of those that a mesh axis runs over, the one named last changes fastest.
Arguments:
- spectra: bfloat16 [256, 256, 512], P(('row', 'col')), may hold values from 0.05 to 20000
- sensor_ids: int32 [256, 1], P(('row', 'col')), may hold values from 0 to 31, as said below
- permutation: int32 [256], P(('row', 'col')), may hold values from 0 to 255, as said below
- w_enc1: bfloat16 [2048, 256], replicated, may hold values from -0.125 to 0.125
- w_enc2: bfloat16 [1024, 256], replicated, may hold values from -0.1875 to 0.1875
- w_dec1: bfloat16 [256, 1024], replicated, may hold values from -0.25 to 0.25
- w_dec2: bfloat16 [256, 2048], replicated, may hold values from -0.25 to 0.25
Outputs:
- grad_enc1: float32 [2048, 256], replicated
- grad_enc2: float32 [1024, 256], replicated
- grad_dec1: float32 [256, 1024], replicated
- grad_dec2: float32 [256, 2048], replicated
The draws below stay inside these ranges and needn't reach their ends.
Inputs may be any that keep to these rules, and one draw needn't show every extreme that they name: `sensor_ids`: every sensor from 0 to 31 recorded exactly 8 windows. A permutation of all slots; the 8 windows of the ingest device with indices (a, b) go to 8 different trainers, one to each trainer whose col index c has c // 2 = a; each trainer thus receives one window from each ingest device of one row index.
All inputs are finite; a program needn't handle non-finite values.
Results may differ from the reference program's by a relative error of at most 0.004.
Values may be sent and summed in bfloat16 or wider, within the bound.
A program may use at most 192 MiB of HBM per device.

```python
import math
import jax
import jax.numpy as jnp
from jax import lax

BINS = 512
CH = 256
WIN_SENSOR = 8
FRAMES = 256
WIN_DEV = 8
PER_ROW = 2
WINDOWS = 256
SENSORS = 32


def sensor_draw(key):
    sensor_key = jax.random.fold_in(key, 11)
    order = jax.random.permutation(sensor_key, WINDOWS)
    return (order // WIN_SENSOR).astype(jnp.int32)


def draw_sensor_ids(key, part):
    return sensor_draw(key)[:, None]


def draw_spectra(key, part):
    first_key, second_key = jax.random.split(key, 2)
    loud_key = jax.random.fold_in(key, 13)
    labels = sensor_draw(key)
    position = jnp.arange(WINDOWS, dtype=jnp.float32) / WINDOWS
    sensor_gain = 10.0 ** jax.random.uniform(loud_key, (SENSORS,), jnp.float32, 0.0, 1.0)
    gain = sensor_gain[labels] * 10.0 ** position
    frame_gain = jnp.exp(jax.random.uniform(first_key, (WINDOWS, FRAMES, 1), jnp.float32, math.log(0.5), math.log(2.0)))
    texture = jnp.exp(jax.random.uniform(second_key, (WINDOWS, FRAMES, BINS), jnp.float32, math.log(0.1), math.log(10.0)))
    return (gain[:, None, None] * frame_gain * texture).astype(jnp.bfloat16)


def draw_permutation(key, part):
    col_total = WIN_DEV
    device_total = WINDOWS // WIN_DEV
    subkeys = jax.random.split(jax.random.fold_in(key, 7), 2)
    offsets = jax.random.randint(subkeys[0], (device_total,), 0, col_total)
    stored = jax.vmap(lambda single: jax.random.permutation(single, col_total))(jax.random.split(subkeys[1], device_total))
    device = jnp.arange(device_total, dtype=jnp.int32)[:, None]
    source_row = device // col_total
    source_col = device % col_total
    dest_row = stored // PER_ROW
    dest_col = source_row * PER_ROW + stored % PER_ROW
    dest_dev = dest_row * col_total + dest_col
    slot = (source_col + offsets[dest_dev]) % col_total
    return (dest_dev * col_total + slot).reshape(-1).astype(jnp.int32)


def scatter_about(rng, extent, spread, most, held_as=jnp.bfloat16):
    values = jax.random.normal(rng, extent, jnp.float32) * spread
    return jnp.minimum(jnp.maximum(values, -most), most).astype(held_as)


def setup_inputs(seed: int = 0) -> dict:
    streams_of = jax.random.split(jax.random.key(seed), 8)
    spectra = draw_spectra(jax.random.fold_in(streams_of[7], 71), 0)
    sensor_ids = draw_sensor_ids(jax.random.fold_in(streams_of[7], 71), 0)
    permutation = draw_permutation(jax.random.fold_in(streams_of[7], 71), 0)
    w_enc1 = scatter_about(streams_of[3], (4 * BINS, CH), (4 * BINS) ** -0.5, 0.125)
    w_enc2 = scatter_about(streams_of[4], (4 * CH, CH), (4 * CH) ** -0.5, 0.1875)
    w_dec1 = scatter_about(streams_of[5], (CH, 4 * CH), (2 * CH) ** -0.5, 0.25)
    w_dec2 = scatter_about(streams_of[6], (CH, 4 * BINS), (2 * CH) ** -0.5, 0.25)
    return dict(spectra=spectra, sensor_ids=sensor_ids, permutation=permutation, w_enc1=w_enc1, w_enc2=w_enc2, w_dec1=w_dec1, w_dec2=w_dec2)


EPS = 1e-05

def frame_taps(values):
    windows, length, channels = values.shape
    padded = jnp.pad(values, ((0, 0), (1, 1), (0, 0)))
    paired = padded.reshape(windows, length // 2 + 1, 2 * channels)
    return jnp.concatenate([paired[:, :-1], paired[:, 1:]], axis=2)

def fold_taps(stacked):
    windows, length, columns = stacked.shape
    channels = columns // 4
    pieces = stacked.reshape(windows, length, 4, channels)
    blank = jnp.zeros((windows, 1, channels), stacked.dtype)
    even_rows = pieces[:, :, 1] + jnp.concatenate([blank, pieces[:, :-1, 3]], axis=1)
    odd_rows = pieces[:, :, 2] + jnp.concatenate([pieces[:, 1:, 0], blank], axis=1)
    return jnp.stack([even_rows, odd_rows], axis=2).reshape(windows, 2 * length, channels)

def silu_slope(values):
    logistic = jax.nn.sigmoid(values)
    return logistic * (1.0 + values * (1.0 - logistic))

def forward_dot(values, weight):
    flat = values.reshape(-1, values.shape[-1]).astype(jnp.float32)
    result = jnp.dot(flat, weight.astype(jnp.float32), precision=lax.Precision.HIGHEST, preferred_element_type=jnp.float32)
    return result.reshape(values.shape[:-1] + (weight.shape[1],))

def backward_dot(values, weight):
    flat = values.reshape(-1, values.shape[-1]).astype(jnp.float32)
    result = jnp.dot(flat, weight.astype(jnp.float32).T, precision=lax.Precision.HIGHEST, preferred_element_type=jnp.float32)
    return result.reshape(values.shape[:-1] + (weight.shape[0],))

def weight_grad(left, right):
    left_flat = left.reshape(-1, left.shape[-1]).astype(jnp.float32)
    right_flat = right.reshape(-1, right.shape[-1]).astype(jnp.float32)
    return jnp.dot(left_flat.T, right_flat, precision=lax.Precision.HIGHEST, preferred_element_type=jnp.float32)

def group_grads(normed, w_enc1, w_enc2, w_dec1, w_dec2):
    stem_taps = frame_taps(normed)
    enc1_pre = forward_dot(stem_taps, w_enc1)
    middle = lax.optimization_barrier(jnp.mean(enc1_pre, axis=(0, 1)))
    variance = lax.optimization_barrier(jnp.mean(jnp.square(enc1_pre - middle), axis=(0, 1)))
    inverse = lax.rsqrt(variance + EPS)
    enc1_hat = (enc1_pre - middle) * inverse
    enc1_out = jax.nn.silu(enc1_hat).astype(jnp.bfloat16)
    mid_taps = frame_taps(enc1_out)
    enc2_pre = forward_dot(mid_taps, w_enc2)
    enc2_out = jax.nn.silu(enc2_pre).astype(jnp.bfloat16)
    dec1_pre = fold_taps(forward_dot(enc2_out, w_dec1))
    dec1_out = jax.nn.silu(dec1_pre).astype(jnp.bfloat16)
    rebuilt = fold_taps(forward_dot(dec1_out, w_dec2))
    delta_out = ((rebuilt - normed.astype(jnp.float32)) / WINDOWS).astype(jnp.bfloat16)
    out_taps = frame_taps(delta_out)
    grad_dec2 = weight_grad(dec1_out, out_taps)
    delta_dec1 = (backward_dot(out_taps, w_dec2) * silu_slope(dec1_pre)).astype(jnp.bfloat16)
    dec_taps = frame_taps(delta_dec1)
    grad_dec1 = weight_grad(enc2_out, dec_taps)
    delta_enc2 = (backward_dot(dec_taps, w_dec1) * silu_slope(enc2_pre)).astype(jnp.bfloat16)
    grad_enc2 = weight_grad(mid_taps, delta_enc2)
    back_enc1 = fold_taps(backward_dot(delta_enc2, w_enc2)) * silu_slope(enc1_hat)
    first_mean = lax.optimization_barrier(jnp.mean(back_enc1, axis=(0, 1)))
    second_mean = lax.optimization_barrier(jnp.mean(back_enc1 * enc1_hat, axis=(0, 1)))
    delta_enc1 = ((back_enc1 - first_mean - enc1_hat * second_mean) * inverse).astype(jnp.bfloat16)
    grad_enc1 = weight_grad(stem_taps, delta_enc1)
    return (grad_enc1, grad_enc2, grad_dec1, grad_dec2)

def reference(spectra, sensor_ids, permutation, w_enc1, w_enc2, w_dec1, w_dec2):
    groups = WINDOWS // WIN_DEV
    sensor = sensor_ids[:, 0].astype(jnp.int32)
    blocks = spectra.reshape(groups, WIN_DEV, FRAMES, BINS)

    def window_stats(block):
        log_power = jnp.log1p(block.astype(jnp.float32))
        return (lax.optimization_barrier(jnp.sum(log_power, axis=1)), lax.optimization_barrier(jnp.sum(log_power * log_power, axis=1)))
    win_sums, win_squares = lax.map(window_stats, blocks)
    win_sums = win_sums.reshape(WINDOWS, BINS)
    win_squares = win_squares.reshape(WINDOWS, BINS)
    totals = jax.ops.segment_sum(win_sums, sensor, num_segments=SENSORS)
    squares = jax.ops.segment_sum(win_squares, sensor, num_segments=SENSORS)
    counts = jax.ops.segment_sum(jnp.ones((WINDOWS,), jnp.float32), sensor, num_segments=SENSORS) * FRAMES
    center = totals / counts[:, None]
    factor = lax.rsqrt(squares / counts[:, None] - center * center + EPS)
    ranking = jnp.argsort(permutation).astype(jnp.int32).reshape(groups, WIN_DEV)

    def group_step(running, members):
        log_power = jnp.log1p(spectra[members].astype(jnp.float32))
        member_ids = sensor[members]
        normed = ((log_power - center[member_ids][:, None, :]) * factor[member_ids][:, None, :]).astype(jnp.bfloat16)
        gradients = group_grads(normed, w_enc1, w_enc2, w_dec1, w_dec2)
        return (tuple((a + b for a, b in zip(running, gradients))), None)
    starts = (jnp.zeros((4 * BINS, CH), jnp.float32), jnp.zeros((4 * CH, CH), jnp.float32), jnp.zeros((CH, 4 * CH), jnp.float32), jnp.zeros((CH, 4 * BINS), jnp.float32))
    result, _ = lax.scan(group_step, starts, ranking)
    return (result[0], result[1], result[2], result[3])
```

```python
import jax
import jax.numpy as jnp
from jax import lax
from jax.sharding import PartitionSpec as P

WIN_SENSOR = 8


EPS = 1e-05


def frame_taps(values):
    windows, length, channels = values.shape
    padded = jnp.pad(values, ((0, 0), (1, 1), (0, 0)))
    paired = padded.reshape(windows, length // 2 + 1, 2 * channels)
    return jnp.concatenate([paired[:, :-1], paired[:, 1:]], axis=2)


def fold_taps(stacked):
    windows, length, columns = stacked.shape
    channels = columns // 4
    pieces = stacked.reshape(windows, length, 4, channels)
    blank = jnp.zeros((windows, 1, channels), stacked.dtype)
    even_rows = pieces[:, :, 1] + jnp.concatenate([blank, pieces[:, :-1, 3]], axis=1)
    odd_rows = pieces[:, :, 2] + jnp.concatenate([pieces[:, 1:, 0], blank], axis=1)
    return jnp.stack([even_rows, odd_rows], axis=2).reshape(windows, 2 * length, channels)


def silu_slope(values):
    logistic = jax.nn.sigmoid(values)
    return logistic * (1.0 + values * (1.0 - logistic))


def forward_dot(values, weight):
    flat = values.reshape(-1, values.shape[-1])
    result = jnp.dot(flat, weight, preferred_element_type=jnp.float32)
    return result.reshape(values.shape[:-1] + (weight.shape[1],))


def backward_dot(values, weight):
    flat = values.reshape(-1, values.shape[-1])
    result = lax.dot_general(
        flat, weight, (((1,), (1,)), ((), ())), preferred_element_type=jnp.float32
    )
    return result.reshape(values.shape[:-1] + (weight.shape[0],))


def sensor_table(sensor_col, sensor_total):
    return (sensor_col[:, None] == jnp.arange(sensor_total, dtype=jnp.int32)[None, :]).astype(
        jnp.float32
    )


def standardize(log_power, table, center, factor):
    shift = jnp.dot(table, center, precision=lax.Precision.HIGHEST)
    stretch = jnp.dot(table, factor, precision=lax.Precision.HIGHEST)
    return ((log_power - shift[:, None, :]) * stretch[:, None, :]).astype(jnp.bfloat16)


def layer_sum(left, right):
    left_flat = left.reshape(-1, left.shape[-1])
    right_flat = right.reshape(-1, right.shape[-1])
    gradient = jnp.einsum("rk,ro->ko", left_flat, right_flat, preferred_element_type=jnp.float32)
    return gradient


def local(spectra, sensor_ids, permutation, w_enc1, w_enc2, w_dec1, w_dec2):
    window_count = spectra.shape[0]
    frame_count = spectra.shape[1]
    row_count = lax.axis_size("row")
    col_count = lax.axis_size("col")
    total_windows = window_count * row_count * col_count
    sensor_total = total_windows // WIN_SENSOR
    per_row = col_count // row_count
    sensor_col = sensor_ids[:, 0]
    trainer = permutation // window_count
    target = trainer // col_count * per_row + trainer % per_row
    ranking = jnp.argsort(target)
    raw = lax.all_to_all(spectra[ranking], "col", split_axis=0, concat_axis=0, tiled=True)
    labels = lax.all_to_all(sensor_col[ranking], "col", split_axis=0, concat_axis=0, tiled=True)
    table = sensor_table(sensor_col, sensor_total)
    log_power = jnp.log1p(spectra.astype(jnp.float32))
    win_sums = jnp.sum(log_power, axis=1)
    win_squares = jnp.sum(log_power * log_power, axis=1)
    totals = jnp.einsum("ws,wb->sb", table, win_sums, precision=lax.Precision.HIGHEST)
    squares = jnp.einsum("ws,wb->sb", table, win_squares, precision=lax.Precision.HIGHEST)
    totals, squares = lax.psum((totals, squares), ("row", "col"))
    count = WIN_SENSOR * frame_count
    center = totals / count
    factor = lax.rsqrt(squares / count - center * center + EPS)
    payload = standardize(
        jnp.log1p(raw.astype(jnp.float32)), sensor_table(labels, sensor_total), center, factor
    )
    stem_taps = frame_taps(payload)
    enc1_pre = forward_dot(stem_taps, w_enc1)
    middle = jnp.mean(enc1_pre, axis=(0, 1))
    variance = jnp.mean(jnp.square(enc1_pre - middle), axis=(0, 1))
    inverse = lax.rsqrt(variance + EPS)
    enc1_hat = (enc1_pre - middle) * inverse
    enc1_out = jax.nn.silu(enc1_hat).astype(jnp.bfloat16)
    mid_taps = frame_taps(enc1_out)
    enc2_pre = forward_dot(mid_taps, w_enc2)
    enc2_out = jax.nn.silu(enc2_pre).astype(jnp.bfloat16)
    dec1_pre = fold_taps(forward_dot(enc2_out, w_dec1))
    dec1_out = jax.nn.silu(dec1_pre).astype(jnp.bfloat16)
    rebuilt = fold_taps(forward_dot(dec1_out, w_dec2))
    delta_out = ((rebuilt - payload.astype(jnp.float32)) / total_windows).astype(jnp.bfloat16)
    out_taps = frame_taps(delta_out)
    grad_dec2 = layer_sum(dec1_out, out_taps)
    delta_dec1 = (backward_dot(out_taps, w_dec2) * silu_slope(dec1_pre)).astype(jnp.bfloat16)
    dec_taps = frame_taps(delta_dec1)
    grad_dec1 = layer_sum(enc2_out, dec_taps)
    delta_enc2 = (backward_dot(dec_taps, w_dec1) * silu_slope(enc2_pre)).astype(jnp.bfloat16)
    grad_enc2 = layer_sum(mid_taps, delta_enc2)
    back_enc1 = fold_taps(backward_dot(delta_enc2, w_enc2)) * silu_slope(enc1_hat)
    first_mean = jnp.mean(back_enc1, axis=(0, 1))
    second_mean = jnp.mean(back_enc1 * enc1_hat, axis=(0, 1))
    delta_enc1 = ((back_enc1 - first_mean - enc1_hat * second_mean) * inverse).astype(jnp.bfloat16)
    grad_enc1 = layer_sum(stem_taps, delta_enc1)
    grads = tuple(
        value.astype(jnp.bfloat16) for value in (grad_enc1, grad_enc2, grad_dec1, grad_dec2)
    )
    grads = lax.psum(grads, ("row", "col"))
    return tuple(value.astype(jnp.float32) for value in grads)


def solution(mesh):
    return jax.shard_map(
        local,
        mesh=mesh,
        in_specs=(
            P(("row", "col"), None, None),
            P(("row", "col"), None),
            P(("row", "col")),
            P(),
            P(),
            P(),
            P(),
        ),
        out_specs=(P(), P(), P(), P()),
        check_vma=False,
    )
```

```python
import functools

import jax
import jax.numpy as jnp
from jax import lax
from jax.experimental import pallas as pl
from jax.experimental.pallas import tpu as pltpu
from jax.sharding import PartitionSpec as P

WIN_SENSOR = 8


EPS = 1e-05
MESH = pl.DeviceIdType.MESH
SEGMENTS = 3
WIDTH = 256


def enter(rows, cols, me_row, me_col):
    barrier = pltpu.get_barrier_semaphore()
    for k in range(1, cols):
        pl.semaphore_signal(
            barrier, inc=1, device_id=(me_row, lax.rem(me_col + k, cols)), device_id_type=MESH
        )
    for k in range(1, rows):
        pl.semaphore_signal(
            barrier, inc=1, device_id=(lax.rem(me_row + k, rows), me_col), device_id_type=MESH
        )
    pl.semaphore_wait(barrier, rows + cols - 2)


def send(src, dst, send_sem, recv_sem, device):
    copy = pltpu.make_async_remote_copy(
        src_ref=src,
        dst_ref=dst,
        send_sem=send_sem,
        recv_sem=recv_sem,
        device_id=device,
        device_id_type=MESH,
    )
    copy.start()
    return copy


def exchange_kernel(
    rows, cols, order_ref, spectra_ref, label_ref, table_ref,
    raw_ref, got_label_ref, stats_ref,
    sorted_buf, sums, part, part_in, share, share_in,
    raw_send, raw_recv, lab_send, lab_recv, a_send, a_recv, b_send, b_recv, c_send, c_recv,
):
    me_row, me_col = lax.axis_index("row"), lax.axis_index("col")
    windows, frames, _ = spectra_ref.shape
    step = 64
    for w in range(windows):
        sorted_buf[w] = spectra_ref[order_ref[w]]
    enter(rows, cols, me_row, me_col)
    copies = []
    for k in range(1, cols):
        peer = lax.rem(me_col + k, cols)
        device = (me_row, peer)
        copies.append(send(sorted_buf.at[peer], raw_ref.at[me_col], raw_send.at[k], raw_recv.at[k], device))
        copies.append(send(label_ref.at[peer], got_label_ref.at[me_col], lab_send.at[k], lab_recv.at[k], device))
    raw_ref[me_col] = sorted_buf[me_col]
    got_label_ref[me_col] = label_ref[me_col]

    def window_sums(w, carry):
        def chunk(i, acc):
            total, square = acc
            values = jnp.log(1.0 + sorted_buf[w, pl.ds(pl.multiple_of(i * step, step), step), :].astype(jnp.float32))
            values = values.reshape(step // 8, 8, values.shape[1])
            return total + jnp.sum(values, axis=0), square + jnp.sum(values * values, axis=0)

        blank = jnp.zeros((8, spectra_ref.shape[2]), jnp.float32)
        total, square = lax.fori_loop(0, frames // step, chunk, (blank, blank))
        sums[w] = jnp.sum(total, axis=0, keepdims=True)
        sums[windows + w] = jnp.sum(square, axis=0, keepdims=True)
        return carry

    lax.fori_loop(0, windows, window_sums, 0)

    def spread(c, carry):
        total = jnp.zeros(part.shape[1:], jnp.float32)
        for w in range(2 * windows):
            total = total + table_ref[c, :, w : w + 1] * sums[w]
        part[c] = total
        return carry

    lax.fori_loop(0, cols, spread, 0)

    first = []
    for k in range(1, cols):
        peer = lax.rem(me_col + k, cols)
        first.append(send(part.at[peer], part_in.at[k], a_send.at[k], a_recv.at[k], (me_row, peer)))
    total = part[me_col]
    for k in range(1, cols):
        first[k - 1].wait_recv()
        total = total + part_in[k]
    share[...] = total
    second = []
    for k in range(1, rows):
        peer = lax.rem(me_row + k, rows)
        second.append(send(share, share_in.at[me_row], b_send.at[k], b_recv.at[k], (peer, me_col)))
    share_in[me_row] = total
    for copy in second:
        copy.wait_recv()
    total = share_in[0]
    for r in range(1, rows):
        total = total + share_in[r]
    stats_ref[me_col] = total
    third = []
    for k in range(1, cols):
        peer = lax.rem(me_col + k, cols)
        third.append(send(stats_ref.at[me_col], stats_ref.at[me_col], c_send.at[k], c_recv.at[k], (me_row, peer)))
    for copy in third + copies:
        copy.wait_recv()
    for copy in first + second + third + copies:
        copy.wait_send()


def exchange(rows, cols, order, spectra, labels, table):
    windows, frames, bins = spectra.shape
    depth = table.shape[1]
    vmem = pl.BlockSpec(memory_space=pltpu.VMEM)
    dma = pltpu.SemaphoreType.DMA
    return pl.pallas_call(
        functools.partial(exchange_kernel, rows, cols),
        out_shape=(
            jax.ShapeDtypeStruct((cols, frames, bins), jnp.bfloat16),
            jax.ShapeDtypeStruct(labels.shape, jnp.int32),
            jax.ShapeDtypeStruct((cols, depth, bins), jnp.float32),
        ),
        in_specs=[pl.BlockSpec(memory_space=pltpu.SMEM), vmem, vmem, vmem],
        out_specs=(vmem, vmem, vmem),
        scratch_shapes=[
            pltpu.VMEM((windows, frames, bins), jnp.bfloat16),
            pltpu.VMEM((2 * windows, 1, bins), jnp.float32),
            pltpu.VMEM((cols, depth, bins), jnp.float32),
            pltpu.VMEM((cols, depth, bins), jnp.float32),
            pltpu.VMEM((depth, bins), jnp.float32),
            pltpu.VMEM((rows, depth, bins), jnp.float32),
        ]
        + [dma((cols,))] * 6 + [dma((rows,))] * 2 + [dma((cols,))] * 2,
        compiler_params=pltpu.CompilerParams(
            collective_id=0, has_side_effects=True, vmem_limit_bytes=48 * 2**20
        ),
    )(order, spectra, labels, table)


class Segment:
    def __init__(self, rows, cols, index, place, src, out, bufs, sems):
        self.rows, self.chips, self.index = rows, cols // 2, index
        self.me_row, self.me_col, self.chip, self.core = place
        self.src, self.out, self.bufs, self.sems = src, out, bufs, sems
        self.open, self.sent = [], []

    def send(self, step, k, src, dst, device):
        send_sem, recv_sem = self.sems[step]
        copy = send(src, dst, send_sem.at[self.index, k], recv_sem.at[self.index, k], device)
        self.open.append(copy)
        self.sent.append(copy)

    def land(self):
        for copy in self.open:
            copy.wait_recv()
        self.open = []

    def step(self, number):
        half_in, quarter, quarter_in, piece, piece_in = (b.at[self.index] for b in self.bufs)
        out, chips, rows = self.out.at[self.index], self.chips, self.rows
        core, chip, me_row = self.core, self.chip, self.me_row
        self.land()
        if number == 0:
            other = 1 - core
            self.send(0, 0, self.src.at[self.index, other], half_in, (me_row, chip * 2 + other))
        elif number == 1:
            def add(q, carry):
                quarter[q] = (self.src[self.index, core, q] + half_in[q]).astype(jnp.bfloat16)
                return carry

            lax.fori_loop(0, chips, add, 0)
            for k in range(1, chips):
                peer = lax.rem(chip + k, chips)
                self.send(1, k, quarter.at[peer], quarter_in.at[k], (me_row, peer * 2 + core))
        elif number == 2:
            def add(r, carry):
                total = self.src[self.index, core, chip, r] + half_in[chip, r]
                for k in range(1, chips):
                    total = total + quarter_in[k, r].astype(jnp.float32)
                piece[r] = total
                return carry

            lax.fori_loop(0, rows, add, 0)
            for k in range(1, rows):
                peer = lax.rem(me_row + k, rows)
                self.send(2, k, piece.at[peer], piece_in.at[k], (peer, self.me_col))
        elif number == 3:
            total = piece[me_row]
            for k in range(1, rows):
                total = total + piece_in[k]
            out[core, chip, me_row] = total.astype(jnp.bfloat16)
            mine = out.at[core, chip, me_row]
            for k in range(1, rows):
                self.send(3, k, mine, mine, (lax.rem(me_row + k, rows), self.me_col))
        elif number == 4:
            mine = out.at[core, chip]
            for k in range(1, chips):
                self.send(4, k, mine, mine, (me_row, lax.rem(chip + k, chips) * 2 + core))
        elif number == 5:
            self.send(5, 0, out.at[core], out.at[core], (me_row, chip * 2 + 1 - core))
        else:
            for copy in self.sent:
                copy.wait_send()


def reduce_kernel(rows, cols, src_ref, out_ref, *scratch):
    me_row, me_col = lax.axis_index("row"), lax.axis_index("col")
    place = (me_row, me_col, me_col // 2, lax.rem(me_col, 2))
    bufs, flat = scratch[:5], scratch[5:]
    sems = [(flat[2 * i], flat[2 * i + 1]) for i in range(6)]
    enter(rows, cols, me_row, me_col)
    segments = [
        Segment(rows, cols, s, place, src_ref, out_ref, bufs, sems) for s in range(SEGMENTS)
    ]
    for time in range(7 + SEGMENTS - 1):
        for s in range(SEGMENTS):
            if 0 <= time - s < 7:
                segments[s].step(time - s)


def reduce_everywhere(rows, cols, stacked):
    chips = cols // 2
    depth = stacked.shape[0] // (SEGMENTS * 2 * chips * rows)
    shape = (SEGMENTS, 2, chips, rows, depth, WIDTH)
    vmem = pl.BlockSpec(memory_space=pltpu.VMEM)
    dma = pltpu.SemaphoreType.DMA
    peers = [1, chips, rows, rows, chips, 1]
    out = pl.pallas_call(
        functools.partial(reduce_kernel, rows, cols),
        out_shape=jax.ShapeDtypeStruct(shape, jnp.bfloat16),
        in_specs=[vmem],
        out_specs=vmem,
        scratch_shapes=[
            pltpu.VMEM((SEGMENTS, chips, rows, depth, WIDTH), jnp.float32),
            pltpu.VMEM((SEGMENTS, chips, rows, depth, WIDTH), jnp.bfloat16),
            pltpu.VMEM((SEGMENTS, chips, rows, depth, WIDTH), jnp.bfloat16),
            pltpu.VMEM((SEGMENTS, rows, depth, WIDTH), jnp.float32),
            pltpu.VMEM((SEGMENTS, rows, depth, WIDTH), jnp.float32),
        ]
        + [dma((SEGMENTS, count)) for count in peers for _ in range(2)],
        compiler_params=pltpu.CompilerParams(
            collective_id=1, has_side_effects=True, vmem_limit_bytes=48 * 2**20
        ),
    )(stacked.reshape(shape))
    return out.reshape(stacked.shape)


def to_rows(value):
    blocks = value.reshape(value.shape[0], -1, WIDTH)
    return jnp.swapaxes(blocks, 0, 1).reshape(-1, WIDTH)


def from_rows(value, height):
    return jnp.swapaxes(value.reshape(-1, height, WIDTH), 0, 1).reshape(height, -1)


def frame_taps(values):
    windows, length, channels = values.shape
    padded = jnp.pad(values, ((0, 0), (1, 1), (0, 0)))
    paired = padded.reshape(windows, length // 2 + 1, 2 * channels)
    return jnp.concatenate([paired[:, :-1], paired[:, 1:]], axis=2)


def fold_taps(stacked):
    windows, length, columns = stacked.shape
    channels = columns // 4
    pieces = stacked.reshape(windows, length, 4, channels)
    blank = jnp.zeros((windows, 1, channels), stacked.dtype)
    even_rows = pieces[:, :, 1] + jnp.concatenate([blank, pieces[:, :-1, 3]], axis=1)
    odd_rows = pieces[:, :, 2] + jnp.concatenate([pieces[:, 1:, 0], blank], axis=1)
    return jnp.stack([even_rows, odd_rows], axis=2).reshape(windows, 2 * length, channels)


def silu_slope(values):
    logistic = jax.nn.sigmoid(values)
    return logistic * (1.0 + values * (1.0 - logistic))


def forward_dot(values, weight):
    flat = values.reshape(-1, values.shape[-1])
    result = jnp.dot(flat, weight, preferred_element_type=jnp.float32)
    return result.reshape(values.shape[:-1] + (weight.shape[1],))


def backward_dot(values, weight):
    flat = values.reshape(-1, values.shape[-1])
    result = lax.dot_general(
        flat, weight, (((1,), (1,)), ((), ())), preferred_element_type=jnp.float32
    )
    return result.reshape(values.shape[:-1] + (weight.shape[0],))


def sensor_table(sensor_col, sensor_total):
    return (sensor_col[:, None] == jnp.arange(sensor_total, dtype=jnp.int32)[None, :]).astype(
        jnp.float32
    )


def standardize(log_power, table, center, factor):
    shift = jnp.dot(table, center, precision=lax.Precision.HIGHEST)
    stretch = jnp.dot(table, factor, precision=lax.Precision.HIGHEST)
    return ((log_power - shift[:, None, :]) * stretch[:, None, :]).astype(jnp.bfloat16)


def layer_sum(left, right):
    left_flat = left.reshape(-1, left.shape[-1])
    right_flat = right.reshape(-1, right.shape[-1])
    gradient = jnp.einsum("rk,ro->ko", left_flat, right_flat, preferred_element_type=jnp.float32)
    return gradient


def local(spectra, sensor_ids, permutation, w_enc1, w_enc2, w_dec1, w_dec2):
    window_count = spectra.shape[0]
    frame_count = spectra.shape[1]
    row_count = lax.axis_size("row")
    col_count = lax.axis_size("col")
    total_windows = window_count * row_count * col_count
    sensor_total = total_windows // WIN_SENSOR
    per_row = col_count // row_count
    sensor_col = sensor_ids[:, 0]
    trainer = permutation // window_count
    target = trainer // col_count * per_row + trainer % per_row
    slots = jnp.arange(window_count, dtype=jnp.int32)
    order = jnp.sum(jnp.where(target[None, :] == slots[:, None], slots[None, :], 0), axis=1)
    owner = jnp.sum(
        jnp.where(target[None, :] == slots[:, None], sensor_col[None, :], 0), axis=1
    )
    per_chunk = sensor_total // col_count
    table = sensor_table(owner, sensor_total).T.reshape(col_count, per_chunk, window_count)
    blank = jnp.zeros_like(table)
    table = jnp.concatenate(
        [
            jnp.concatenate([table, blank], axis=2),
            jnp.concatenate([blank, table], axis=2),
        ],
        axis=1,
    )
    labels = jnp.broadcast_to(owner[:, None, None], (window_count, 8, 128))
    raw, labels, stats = exchange(row_count, col_count, order, spectra, labels, table)
    stats = stats.reshape(col_count, 2, per_chunk, -1)
    totals = stats[:, 0].reshape(sensor_total, -1)
    squares = stats[:, 1].reshape(sensor_total, -1)
    count = WIN_SENSOR * frame_count
    center = totals / count
    factor = lax.rsqrt(squares / count - center * center + EPS)
    payload = standardize(
        jnp.log1p(raw.astype(jnp.float32)),
        sensor_table(labels[:, 0, 0], sensor_total),
        center,
        factor,
    )
    stem_taps = frame_taps(payload)
    enc1_pre = forward_dot(stem_taps, w_enc1)
    middle = jnp.mean(enc1_pre, axis=(0, 1))
    variance = jnp.mean(jnp.square(enc1_pre - middle), axis=(0, 1))
    inverse = lax.rsqrt(variance + EPS)
    enc1_hat = (enc1_pre - middle) * inverse
    enc1_out = jax.nn.silu(enc1_hat).astype(jnp.bfloat16)
    mid_taps = frame_taps(enc1_out)
    enc2_pre = forward_dot(mid_taps, w_enc2)
    enc2_out = jax.nn.silu(enc2_pre).astype(jnp.bfloat16)
    dec1_pre = fold_taps(forward_dot(enc2_out, w_dec1))
    dec1_out = jax.nn.silu(dec1_pre).astype(jnp.bfloat16)
    rebuilt = fold_taps(forward_dot(dec1_out, w_dec2))
    delta_out = ((rebuilt - payload.astype(jnp.float32)) / total_windows).astype(jnp.bfloat16)
    out_taps = frame_taps(delta_out)
    grad_dec2 = layer_sum(dec1_out, out_taps)
    delta_dec1 = (backward_dot(out_taps, w_dec2) * silu_slope(dec1_pre)).astype(jnp.bfloat16)
    dec_taps = frame_taps(delta_dec1)
    grad_dec1 = layer_sum(enc2_out, dec_taps)
    delta_enc2 = (backward_dot(dec_taps, w_dec1) * silu_slope(enc2_pre)).astype(jnp.bfloat16)
    grad_enc2 = layer_sum(mid_taps, delta_enc2)
    back_enc1 = fold_taps(backward_dot(delta_enc2, w_enc2)) * silu_slope(enc1_hat)
    first_mean = jnp.mean(back_enc1, axis=(0, 1))
    second_mean = jnp.mean(back_enc1 * enc1_hat, axis=(0, 1))
    delta_enc1 = ((back_enc1 - first_mean - enc1_hat * second_mean) * inverse).astype(jnp.bfloat16)
    grad_enc1 = layer_sum(stem_taps, delta_enc1)
    stacked = jnp.concatenate(
        [
            to_rows(value)
            for value in (grad_dec2, grad_dec1, grad_enc2, grad_enc1)
        ]
    )
    stacked = reduce_everywhere(row_count, col_count, stacked).astype(jnp.float32)
    grads, start = [], 0
    for value in (grad_dec2, grad_dec1, grad_enc2, grad_enc1):
        stop = start + value.size // WIDTH
        grads.append(from_rows(stacked[start:stop], value.shape[0]))
        start = stop
    return tuple(grads[::-1])


def solution(mesh):
    return jax.shard_map(
        local,
        mesh=mesh,
        in_specs=(
            P(("row", "col"), None, None),
            P(("row", "col"), None),
            P(("row", "col")),
            P(),
            P(),
            P(),
            P(),
        ),
        out_specs=(P(), P(), P(), P()),
        check_vma=False,
    )
```

```python
import functools

import jax
import jax.numpy as jnp
from jax import lax
from jax.experimental import pallas as pl
from jax.experimental.pallas import tpu as pltpu
from jax.sharding import PartitionSpec as P

WIN_SENSOR = 8


EPS = 1e-05
MESH = pl.DeviceIdType.MESH
SEGMENTS = 3
WIDTH = 256


def enter(rows, cols, me_row, me_col):
    barrier = pltpu.get_barrier_semaphore()
    for k in range(1, cols):
        pl.semaphore_signal(
            barrier, inc=1, device_id=(me_row, lax.rem(me_col + k, cols)), device_id_type=MESH
        )
    for k in range(1, rows):
        pl.semaphore_signal(
            barrier, inc=1, device_id=(lax.rem(me_row + k, rows), me_col), device_id_type=MESH
        )
    pl.semaphore_wait(barrier, rows + cols - 2)


def send(src, dst, send_sem, recv_sem, device):
    copy = pltpu.make_async_remote_copy(
        src_ref=src,
        dst_ref=dst,
        send_sem=send_sem,
        recv_sem=recv_sem,
        device_id=device,
        device_id_type=MESH,
    )
    copy.start()
    return copy


def exchange_kernel(
    rows, cols, order_ref, spectra_ref, label_ref, table_ref,
    raw_ref, got_label_ref, stats_ref,
    sorted_buf, sums, part, part_in, share, share_in,
    raw_send, raw_recv, lab_send, lab_recv, a_send, a_recv, b_send, b_recv, c_send, c_recv,
):
    me_row, me_col = lax.axis_index("row"), lax.axis_index("col")
    windows, frames, _ = spectra_ref.shape
    step = 64
    for w in range(windows):
        sorted_buf[w] = spectra_ref[order_ref[w]]
    enter(rows, cols, me_row, me_col)
    copies = []
    for k in range(1, cols):
        peer = lax.rem(me_col + k, cols)
        device = (me_row, peer)
        copies.append(send(sorted_buf.at[peer], raw_ref.at[me_col], raw_send.at[k], raw_recv.at[k], device))
        copies.append(send(label_ref.at[peer], got_label_ref.at[me_col], lab_send.at[k], lab_recv.at[k], device))
    raw_ref[me_col] = sorted_buf[me_col]
    got_label_ref[me_col] = label_ref[me_col]

    def window_sums(w, carry):
        def chunk(i, acc):
            total, square = acc
            values = jnp.log(1.0 + sorted_buf[w, pl.ds(pl.multiple_of(i * step, step), step), :].astype(jnp.float32))
            values = values.reshape(step // 8, 8, values.shape[1])
            return total + jnp.sum(values, axis=0), square + jnp.sum(values * values, axis=0)

        blank = jnp.zeros((8, spectra_ref.shape[2]), jnp.float32)
        total, square = lax.fori_loop(0, frames // step, chunk, (blank, blank))
        sums[w] = jnp.sum(total, axis=0, keepdims=True)
        sums[windows + w] = jnp.sum(square, axis=0, keepdims=True)
        return carry

    lax.fori_loop(0, windows, window_sums, 0)

    def spread(c, carry):
        total = jnp.zeros(part.shape[1:], jnp.float32)
        for w in range(2 * windows):
            total = total + table_ref[c, :, w : w + 1] * sums[w]
        part[c] = total
        return carry

    lax.fori_loop(0, cols, spread, 0)

    first = []
    for k in range(1, cols):
        peer = lax.rem(me_col + k, cols)
        first.append(send(part.at[peer], part_in.at[k], a_send.at[k], a_recv.at[k], (me_row, peer)))
    total = part[me_col]
    for k in range(1, cols):
        first[k - 1].wait_recv()
        total = total + part_in[k]
    share[...] = total
    second = []
    for k in range(1, rows):
        peer = lax.rem(me_row + k, rows)
        second.append(send(share, share_in.at[me_row], b_send.at[k], b_recv.at[k], (peer, me_col)))
    share_in[me_row] = total
    for copy in second:
        copy.wait_recv()
    total = share_in[0]
    for r in range(1, rows):
        total = total + share_in[r]
    stats_ref[me_col] = total
    third = []
    for k in range(1, cols):
        peer = lax.rem(me_col + k, cols)
        third.append(send(stats_ref.at[me_col], stats_ref.at[me_col], c_send.at[k], c_recv.at[k], (me_row, peer)))
    for copy in third + copies:
        copy.wait_recv()
    for copy in first + second + third + copies:
        copy.wait_send()


def exchange(rows, cols, order, spectra, labels, table):
    windows, frames, bins = spectra.shape
    depth = table.shape[1]
    vmem = pl.BlockSpec(memory_space=pltpu.VMEM)
    dma = pltpu.SemaphoreType.DMA
    return pl.pallas_call(
        functools.partial(exchange_kernel, rows, cols),
        out_shape=(
            jax.ShapeDtypeStruct((cols, frames, bins), jnp.bfloat16),
            jax.ShapeDtypeStruct(labels.shape, jnp.int32),
            jax.ShapeDtypeStruct((cols, depth, bins), jnp.float32),
        ),
        in_specs=[pl.BlockSpec(memory_space=pltpu.SMEM), vmem, vmem, vmem],
        out_specs=(vmem, vmem, vmem),
        scratch_shapes=[
            pltpu.VMEM((windows, frames, bins), jnp.bfloat16),
            pltpu.VMEM((2 * windows, 1, bins), jnp.float32),
            pltpu.VMEM((cols, depth, bins), jnp.float32),
            pltpu.VMEM((cols, depth, bins), jnp.float32),
            pltpu.VMEM((depth, bins), jnp.float32),
            pltpu.VMEM((rows, depth, bins), jnp.float32),
        ]
        + [dma((cols,))] * 6 + [dma((rows,))] * 2 + [dma((cols,))] * 2,
        compiler_params=pltpu.CompilerParams(
            collective_id=0, has_side_effects=True, vmem_limit_bytes=48 * 2**20
        ),
    )(order, spectra, labels, table)


class Segment:
    def __init__(self, rows, cols, index, place, src, out, bufs, sems):
        self.rows, self.chips, self.index = rows, cols // 2, index
        self.me_row, self.me_col, self.chip, self.core = place
        self.src, self.out, self.bufs, self.sems = src, out, bufs, sems
        self.open, self.sent = [], []

    def send(self, step, k, src, dst, device):
        send_sem, recv_sem = self.sems[step]
        copy = send(src, dst, send_sem.at[self.index, k], recv_sem.at[self.index, k], device)
        self.open.append(copy)
        self.sent.append(copy)

    def land(self):
        for copy in self.open:
            copy.wait_recv()
        self.open = []

    def step(self, number):
        half_in, quarter, quarter_in, piece, piece_in = (b.at[self.index] for b in self.bufs)
        out, chips, rows = self.out.at[self.index], self.chips, self.rows
        core, chip, me_row = self.core, self.chip, self.me_row
        self.land()
        if number == 0:
            other = 1 - core
            self.send(0, 0, self.src.at[self.index, other], half_in, (me_row, chip * 2 + other))
        elif number == 1:
            def add(q, carry):
                quarter[q] = (self.src[self.index, core, q] + half_in[q]).astype(jnp.bfloat16)
                return carry

            lax.fori_loop(0, chips, add, 0)
            for k in range(1, chips):
                peer = lax.rem(chip + k, chips)
                self.send(1, k, quarter.at[peer], quarter_in.at[k], (me_row, peer * 2 + core))
        elif number == 2:
            def add(r, carry):
                total = self.src[self.index, core, chip, r] + half_in[chip, r]
                for k in range(1, chips):
                    total = total + quarter_in[k, r].astype(jnp.float32)
                piece[r] = total
                return carry

            lax.fori_loop(0, rows, add, 0)
            for k in range(1, rows):
                peer = lax.rem(me_row + k, rows)
                self.send(2, k, piece.at[peer], piece_in.at[k], (peer, self.me_col))
        elif number == 3:
            total = piece[me_row]
            for k in range(1, rows):
                total = total + piece_in[k]
            out[core, chip, me_row] = total.astype(jnp.bfloat16)
            mine = out.at[core, chip, me_row]
            for k in range(1, rows):
                self.send(3, k, mine, mine, (lax.rem(me_row + k, rows), self.me_col))
        elif number == 4:
            mine = out.at[core, chip]
            for k in range(1, chips):
                self.send(4, k, mine, mine, (me_row, lax.rem(chip + k, chips) * 2 + core))
        elif number == 5:
            self.send(5, 0, out.at[core], out.at[core], (me_row, chip * 2 + 1 - core))
        else:
            for copy in self.sent:
                copy.wait_send()


def reduce_kernel(rows, cols, src_ref, out_ref, *scratch):
    me_row, me_col = lax.axis_index("row"), lax.axis_index("col")
    place = (me_row, me_col, me_col // 2, lax.rem(me_col, 2))
    bufs, flat = scratch[:5], scratch[5:]
    sems = [(flat[2 * i], flat[2 * i + 1]) for i in range(6)]
    enter(rows, cols, me_row, me_col)
    segments = [
        Segment(rows, cols, s, place, src_ref, out_ref, bufs, sems) for s in range(SEGMENTS)
    ]
    for time in range(7 + SEGMENTS - 1):
        for s in range(SEGMENTS):
            if 0 <= time - s < 7:
                segments[s].step(time - s)


def reduce_everywhere(rows, cols, stacked):
    chips = cols // 2
    depth = stacked.shape[0] // (SEGMENTS * 2 * chips * rows)
    shape = (SEGMENTS, 2, chips, rows, depth, WIDTH)
    vmem = pl.BlockSpec(memory_space=pltpu.VMEM)
    dma = pltpu.SemaphoreType.DMA
    peers = [1, chips, rows, rows, chips, 1]
    out = pl.pallas_call(
        functools.partial(reduce_kernel, rows, cols),
        out_shape=jax.ShapeDtypeStruct(shape, jnp.bfloat16),
        in_specs=[vmem],
        out_specs=vmem,
        scratch_shapes=[
            pltpu.VMEM((SEGMENTS, chips, rows, depth, WIDTH), jnp.float32),
            pltpu.VMEM((SEGMENTS, chips, rows, depth, WIDTH), jnp.bfloat16),
            pltpu.VMEM((SEGMENTS, chips, rows, depth, WIDTH), jnp.bfloat16),
            pltpu.VMEM((SEGMENTS, rows, depth, WIDTH), jnp.float32),
            pltpu.VMEM((SEGMENTS, rows, depth, WIDTH), jnp.float32),
        ]
        + [dma((SEGMENTS, count)) for count in peers for _ in range(2)],
        compiler_params=pltpu.CompilerParams(
            collective_id=1, has_side_effects=True, vmem_limit_bytes=48 * 2**20
        ),
    )(stacked.reshape(shape))
    return out.reshape(stacked.shape)


def from_rows(value, height):
    return jnp.swapaxes(value.reshape(-1, height, WIDTH), 0, 1).reshape(height, -1)


VFRAMES = 64


def dot(left, right, dims):
    return lax.dot_general(left, right, (dims, ((), ())), preferred_element_type=jnp.float32)


AB = ((1,), (0,))
ABT = ((1,), (1,))
ATB = ((0,), (0,))


def earlier(values):
    row = lax.broadcasted_iota(jnp.int32, values.shape, 0)
    return jnp.where(lax.rem(row, VFRAMES) == 0, 0.0, pltpu.roll(values, 1, 0))


def later(values):
    row = lax.broadcasted_iota(jnp.int32, values.shape, 0)
    return jnp.where(
        lax.rem(row, VFRAMES) == VFRAMES - 1, 0.0, pltpu.roll(values, values.shape[0] - 1, 0)
    )


def logistic(values):
    return 1.0 / (1.0 + jnp.exp(-values))


def silu_slope(values):
    gate = logistic(values)
    return gate * (1.0 + values * (1.0 - gate))


def train_kernel(
    total_windows, id_ref, raw_ref, stats_ref, w1_ref, w2_ref, w3_ref, w4_ref, out_ref,
    plain, xb, db, pre, hat0, hat1, ab, enc2, bb, dec0, dec1, d0, d1, eb, fb, g0, g1,
):
    windows, frames, bins = raw_ref.shape
    rows = windows * VFRAMES
    ch = WIDTH
    block = min(rows, 256)
    per_chunk = stats_ref.shape[1] // 2
    count = WIN_SENSOR * frames
    bf = jnp.bfloat16

    def each_block(body):
        def run(i, carry):
            body(pl.ds(pl.multiple_of(i * block, block), block))
            return carry

        lax.fori_loop(0, rows // block, run, 0)

    def normalize(w, carry):
        sensor = id_ref[w]
        chunk, inner = sensor // per_chunk, lax.rem(sensor, per_chunk)
        center = stats_ref[chunk, pl.ds(inner, 1), :] / count
        square = stats_ref[chunk, pl.ds(per_chunk + inner, 1), :] / count
        factor = lax.rsqrt(square - center * center + EPS)
        for i in range(4):
            part = pl.ds(i * (frames // 4), frames // 4)
            value = (jnp.log(1.0 + raw_ref[w, part, :].astype(jnp.float32)) - center) * factor
            for c in range(4):
                plain[c, part, :] = value[:, c * 128 : (c + 1) * 128]
        at = pl.ds(pl.multiple_of(w * VFRAMES, VFRAMES), VFRAMES)
        for c in range(4):
            quarter = [plain[c, pl.ds(p, VFRAMES, stride=4), :] for p in range(4)]
            six = [earlier(quarter[3])] + quarter + [later(quarter[0])]
            for p in range(6):
                start = p * bins + c * 128
                xb[at, start : start + 128] = six[p].astype(bf)
        return carry

    lax.fori_loop(0, windows, normalize, 0)

    def first_layer(at):
        for q in range(2):
            pre[q, at, :] = dot(xb[at, 1024 * q : 1024 * q + 2048], w1_ref[...], AB)

    each_block(first_layer)
    mean = jnp.sum(pre[0] + pre[1], axis=0, keepdims=True) / (2 * rows)
    spread = jnp.square(pre[0] - mean) + jnp.square(pre[1] - mean)
    inverse = lax.rsqrt(jnp.sum(spread, axis=0, keepdims=True) / (2 * rows) + EPS)

    def forward(at):
        h0 = (pre[0, at, :] - mean) * inverse
        h1 = (pre[1, at, :] - mean) * inverse
        hat0[at, :] = h0
        hat1[at, :] = h1
        a0, a1 = h0 * logistic(h0), h1 * logistic(h1)
        for i, value in enumerate((earlier(a1), a0, a1, later(a0))):
            ab[at, i * ch : (i + 1) * ch] = value.astype(bf)
        e = dot(ab[at, :], w2_ref[...], AB)
        enc2[at, :] = e
        low = (e * logistic(e)).astype(bf)
        bb[at, :] = low
        z = [dot(low, w3_ref[:, i * ch : (i + 1) * ch], AB) for i in range(4)]
        p0, p1 = z[1] + earlier(z[3]), z[2] + later(z[0])
        dec0[at, :] = p0
        dec1[at, :] = p1
        o0, o1 = (p0 * logistic(p0)).astype(bf), (p1 * logistic(p1)).astype(bf)
        d0[at, :] = o0
        d1[at, :] = o1
        for c in range(bins // 256):
            def y(value, i):
                start = i * bins + c * 256
                return dot(value, w4_ref[:, start : start + 256], AB)

            rebuilt = (
                y(o0, 1) + earlier(y(o1, 3)),
                y(o0, 2) + y(o1, 0),
                y(o1, 1) + y(o0, 3),
                y(o1, 2) + later(y(o0, 0)),
            )
            delta = []
            for p in range(4):
                start = (p + 1) * bins + c * 256
                normed = xb[at, start : start + 256].astype(jnp.float32)
                delta.append((rebuilt[p] - normed) / total_windows)
            six = [earlier(delta[3])] + delta + [later(delta[0])]
            for p in range(6):
                start = p * bins + c * 256
                db[at, start : start + 256] = six[p].astype(bf)

    each_block(forward)

    def grad_dec2(i, carry):
        left = pl.ds(pl.multiple_of(i * ch, ch), ch)
        right = pl.ds(pl.multiple_of(2 * bins + i * ch, ch), ch)
        out_ref[left, :] = dot(d0[...], db[:, left], ATB) + dot(d1[...], db[:, right], ATB)
        return carry

    lax.fori_loop(0, 4 * bins // ch, grad_dec2, 0)

    def backward(at):
        e0 = dot(db[at, 0:2048], w4_ref[...], ABT) * silu_slope(dec0[at, :])
        e1 = dot(db[at, 1024:3072], w4_ref[...], ABT) * silu_slope(dec1[at, :])
        for i, value in enumerate((earlier(e1), e0, e1, later(e0))):
            eb[at, i * ch : (i + 1) * ch] = value.astype(bf)
        f = (dot(eb[at, :], w3_ref[...], ABT) * silu_slope(enc2[at, :])).astype(bf)
        fb[at, :] = f
        z = [dot(f, w2_ref[i * ch : (i + 1) * ch, :], ABT) for i in range(4)]
        pre[0, at, :] = (z[1] + earlier(z[3])) * silu_slope(hat0[at, :])
        pre[1, at, :] = (z[2] + later(z[0])) * silu_slope(hat1[at, :])

    each_block(backward)
    base = 4 * bins
    for i in range(4):
        out_ref[base + i * ch : base + (i + 1) * ch, :] = dot(bb[...], eb[:, i * ch : (i + 1) * ch], ATB)
    base += 4 * ch
    for i in range(4):
        out_ref[base + i * ch : base + (i + 1) * ch, :] = dot(ab[:, i * ch : (i + 1) * ch], fb[...], ATB)
    base += 4 * ch
    first = jnp.sum(pre[0] + pre[1], axis=0, keepdims=True) / (2 * rows)
    second = jnp.sum(pre[0] * hat0[...] + pre[1] * hat1[...], axis=0, keepdims=True) / (2 * rows)

    def last(at):
        g0[at, :] = ((pre[0, at, :] - first - hat0[at, :] * second) * inverse).astype(bf)
        g1[at, :] = ((pre[1, at, :] - first - hat1[at, :] * second) * inverse).astype(bf)

    each_block(last)

    def grad_enc1(i, carry):
        left = pl.ds(pl.multiple_of(i * ch, ch), ch)
        right = pl.ds(pl.multiple_of(2 * bins + i * ch, ch), ch)
        to = pl.ds(pl.multiple_of(base + i * ch, ch), ch)
        out_ref[to, :] = dot(xb[:, left], g0[...], ATB) + dot(xb[:, right], g1[...], ATB)
        return carry

    lax.fori_loop(0, 4 * bins // ch, grad_enc1, 0)


def train(total_windows, ids, raw, stats, w_enc1, w_enc2, w_dec1, w_dec2):
    windows, frames, bins = raw.shape
    rows = windows * VFRAMES
    vmem = pl.BlockSpec(memory_space=pltpu.VMEM)

    def wide(columns):
        return pltpu.VMEM((rows, columns), jnp.bfloat16)

    def full(columns):
        return pltpu.VMEM((rows, columns), jnp.float32)

    return pl.pallas_call(
        functools.partial(train_kernel, total_windows),
        out_shape=jax.ShapeDtypeStruct((8 * bins + 8 * WIDTH, WIDTH), jnp.float32),
        in_specs=[pl.BlockSpec(memory_space=pltpu.SMEM)] + [vmem] * 6,
        out_specs=vmem,
        scratch_shapes=[
            pltpu.VMEM((4, frames, 128), jnp.float32),
            wide(6 * bins),
            wide(6 * bins),
            pltpu.VMEM((2, rows, WIDTH), jnp.float32),
            full(WIDTH), full(WIDTH),
            wide(4 * WIDTH),
            full(WIDTH),
            wide(WIDTH),
            full(WIDTH), full(WIDTH),
            wide(WIDTH), wide(WIDTH),
            wide(4 * WIDTH),
            wide(WIDTH), wide(WIDTH), wide(WIDTH),
        ],
        compiler_params=pltpu.CompilerParams(vmem_limit_bytes=56 * 2**20),
    )(ids, raw, stats, w_enc1, w_enc2, w_dec1, w_dec2)


def sensor_table(sensor_col, sensor_total):
    return (sensor_col[:, None] == jnp.arange(sensor_total, dtype=jnp.int32)[None, :]).astype(
        jnp.float32
    )


def local(spectra, sensor_ids, permutation, w_enc1, w_enc2, w_dec1, w_dec2):
    window_count = spectra.shape[0]
    frame_count = spectra.shape[1]
    row_count = lax.axis_size("row")
    col_count = lax.axis_size("col")
    total_windows = window_count * row_count * col_count
    sensor_total = total_windows // WIN_SENSOR
    per_row = col_count // row_count
    sensor_col = sensor_ids[:, 0]
    trainer = permutation // window_count
    target = trainer // col_count * per_row + trainer % per_row
    slots = jnp.arange(window_count, dtype=jnp.int32)
    order = jnp.sum(jnp.where(target[None, :] == slots[:, None], slots[None, :], 0), axis=1)
    owner = jnp.sum(
        jnp.where(target[None, :] == slots[:, None], sensor_col[None, :], 0), axis=1
    )
    per_chunk = sensor_total // col_count
    table = sensor_table(owner, sensor_total).T.reshape(col_count, per_chunk, window_count)
    blank = jnp.zeros_like(table)
    table = jnp.concatenate(
        [
            jnp.concatenate([table, blank], axis=2),
            jnp.concatenate([blank, table], axis=2),
        ],
        axis=1,
    )
    labels = jnp.broadcast_to(owner[:, None, None], (window_count, 8, 128))
    raw, labels, stats = exchange(row_count, col_count, order, spectra, labels, table)
    stacked = train(
        total_windows, labels[:, 0, 0], raw, stats, w_enc1, w_enc2, w_dec1, w_dec2
    )
    stacked = reduce_everywhere(row_count, col_count, stacked).astype(jnp.float32)
    grads, start = [], 0
    for weight in (w_dec2, w_dec1, w_enc2, w_enc1):
        stop = start + weight.size // WIDTH
        grads.append(from_rows(stacked[start:stop], weight.shape[0]))
        start = stop
    return tuple(grads[::-1])


def solution(mesh):
    return jax.shard_map(
        local,
        mesh=mesh,
        in_specs=(
            P(("row", "col"), None, None),
            P(("row", "col"), None),
            P(("row", "col")),
            P(),
            P(),
            P(),
            P(),
        ),
        out_specs=(P(), P(), P(), P()),
        check_vma=False,
    )
```

```python
import functools

import jax
import jax.numpy as jnp
from jax import lax
from jax.experimental import pallas as pl
from jax.experimental.pallas import tpu as pltpu
from jax.sharding import PartitionSpec as P

WIN_SENSOR = 8


EPS = 1e-05
MESH = pl.DeviceIdType.MESH
WIDTH = 256


def enter(rows, cols, me_row, me_col):
    barrier = pltpu.get_barrier_semaphore()
    for k in range(1, cols):
        pl.semaphore_signal(
            barrier, inc=1, device_id=(me_row, lax.rem(me_col + k, cols)), device_id_type=MESH
        )
    for k in range(1, rows):
        pl.semaphore_signal(
            barrier, inc=1, device_id=(lax.rem(me_row + k, rows), me_col), device_id_type=MESH
        )
    pl.semaphore_wait(barrier, rows + cols - 2)


def send(src, dst, send_sem, recv_sem, device):
    copy = pltpu.make_async_remote_copy(
        src_ref=src,
        dst_ref=dst,
        send_sem=send_sem,
        recv_sem=recv_sem,
        device_id=device,
        device_id_type=MESH,
    )
    copy.start()
    return copy


def exchange_kernel(
    rows, cols, order_ref, spectra_ref, label_ref, table_ref,
    raw_ref, got_label_ref, stats_ref,
    sorted_buf, sums, part, part_in, share, share_in,
    raw_send, raw_recv, lab_send, lab_recv, a_send, a_recv, b_send, b_recv, c_send, c_recv,
):
    me_row, me_col = lax.axis_index("row"), lax.axis_index("col")
    windows, frames, _ = spectra_ref.shape
    step = 64
    for w in range(windows):
        sorted_buf[w] = spectra_ref[order_ref[w]]
    enter(rows, cols, me_row, me_col)
    copies = []

    def batch(number, start, size):
        part = pl.ds(start, size)
        for k in range(1, cols):
            peer = lax.rem(me_col + k, cols)
            copies.append(
                send(
                    sorted_buf.at[peer, part], raw_ref.at[me_col, part],
                    raw_send.at[number, k], raw_recv.at[number, k], (me_row, peer),
                )
            )

    batch(0, 0, frames // 2)
    for k in range(1, cols):
        peer = lax.rem(me_col + k, cols)
        device = (me_row, peer)
        copies.append(send(label_ref.at[peer], got_label_ref.at[me_col], lab_send.at[k], lab_recv.at[k], device))
    raw_ref[me_col] = sorted_buf[me_col]
    got_label_ref[me_col] = label_ref[me_col]

    def window_sums(w, carry):
        def chunk(i, acc):
            total, square = acc
            values = jnp.log(1.0 + sorted_buf[w, pl.ds(pl.multiple_of(i * step, step), step), :].astype(jnp.float32))
            values = values.reshape(step // 8, 8, values.shape[1])
            return total + jnp.sum(values, axis=0), square + jnp.sum(values * values, axis=0)

        blank = jnp.zeros((8, spectra_ref.shape[2]), jnp.float32)
        total, square = lax.fori_loop(0, frames // step, chunk, (blank, blank))
        sums[w] = jnp.sum(total, axis=0, keepdims=True)
        sums[windows + w] = jnp.sum(square, axis=0, keepdims=True)
        return carry

    lax.fori_loop(0, windows, window_sums, 0)

    def spread(c, carry):
        total = jnp.zeros(part.shape[1:], jnp.float32)
        for w in range(2 * windows):
            total = total + table_ref[c, :, w : w + 1] * sums[w]
        part[c] = total
        return carry

    lax.fori_loop(0, cols, spread, 0)

    first = []
    for k in range(1, cols):
        peer = lax.rem(me_col + k, cols)
        first.append(send(part.at[peer], part_in.at[k], a_send.at[k], a_recv.at[k], (me_row, peer)))
    batch(1, frames // 2, frames // 4)
    total = part[me_col]
    for k in range(1, cols):
        first[k - 1].wait_recv()
        total = total + part_in[k]
    share[...] = total
    second = []
    for k in range(1, rows):
        peer = lax.rem(me_row + k, rows)
        second.append(send(share, share_in.at[me_row], b_send.at[k], b_recv.at[k], (peer, me_col)))
    share_in[me_row] = total
    for copy in second:
        copy.wait_recv()
    total = share_in[0]
    for r in range(1, rows):
        total = total + share_in[r]
    stats_ref[me_col] = total
    third = []
    for k in range(1, cols):
        peer = lax.rem(me_col + k, cols)
        third.append(send(stats_ref.at[me_col], stats_ref.at[me_col], c_send.at[k], c_recv.at[k], (me_row, peer)))
    batch(2, frames // 2 + frames // 4, frames // 4)
    for copy in third + copies:
        copy.wait_recv()
    for copy in first + second + third + copies:
        copy.wait_send()


def exchange(rows, cols, order, spectra, labels, table):
    windows, frames, bins = spectra.shape
    depth = table.shape[1]
    vmem = pl.BlockSpec(memory_space=pltpu.VMEM)
    dma = pltpu.SemaphoreType.DMA
    return pl.pallas_call(
        functools.partial(exchange_kernel, rows, cols),
        out_shape=(
            jax.ShapeDtypeStruct((cols, frames, bins), jnp.bfloat16),
            jax.ShapeDtypeStruct(labels.shape, jnp.int32),
            jax.ShapeDtypeStruct((cols, depth, bins), jnp.float32),
        ),
        in_specs=[pl.BlockSpec(memory_space=pltpu.SMEM), vmem, vmem, vmem],
        out_specs=(vmem, vmem, vmem),
        scratch_shapes=[
            pltpu.VMEM((windows, frames, bins), jnp.bfloat16),
            pltpu.VMEM((2 * windows, 1, bins), jnp.float32),
            pltpu.VMEM((cols, depth, bins), jnp.float32),
            pltpu.VMEM((cols, depth, bins), jnp.float32),
            pltpu.VMEM((depth, bins), jnp.float32),
            pltpu.VMEM((rows, depth, bins), jnp.float32),
        ]
        + [dma((3, cols))] * 2 + [dma((cols,))] * 4 + [dma((rows,))] * 2 + [dma((cols,))] * 2,
        compiler_params=pltpu.CompilerParams(
            collective_id=0, has_side_effects=True, vmem_limit_bytes=48 * 2**20
        ),
    )(order, spectra, labels, table)


class Segment:
    def __init__(self, rows, cols, index, place, src, out, bufs, sems):
        self.rows, self.chips, self.index = rows, cols // 2, index
        self.me_row, self.me_col, self.chip, self.core = place
        self.src, self.out, self.bufs, self.sems = src, out, bufs, sems
        self.open, self.sent = [], []

    def send(self, step, k, src, dst, device):
        send_sem, recv_sem = self.sems[step]
        copy = send(src, dst, send_sem.at[self.index, k], recv_sem.at[self.index, k], device)
        self.open.append(copy)
        self.sent.append(copy)

    def land(self):
        for copy in self.open:
            copy.wait_recv()
        self.open = []

    def step(self, number):
        half_in, quarter, quarter_in, piece, piece_in = (b.at[self.index] for b in self.bufs)
        out, chips, rows = self.out.at[self.index], self.chips, self.rows
        core, chip, me_row = self.core, self.chip, self.me_row
        self.land()
        if number == 0:
            other = 1 - core
            self.send(0, 0, self.src.at[self.index, other], half_in, (me_row, chip * 2 + other))
        elif number == 1:
            def add(q, carry):
                quarter[q] = (self.src[self.index, core, q] + half_in[q]).astype(jnp.bfloat16)
                return carry

            lax.fori_loop(0, chips, add, 0)
            for k in range(1, chips):
                peer = lax.rem(chip + k, chips)
                self.send(1, k, quarter.at[peer], quarter_in.at[k], (me_row, peer * 2 + core))
        elif number == 2:
            def add(r, carry):
                total = self.src[self.index, core, chip, r] + half_in[chip, r]
                for k in range(1, chips):
                    total = total + quarter_in[k, r].astype(jnp.float32)
                piece[r] = total
                return carry

            lax.fori_loop(0, rows, add, 0)
            for k in range(1, rows):
                peer = lax.rem(me_row + k, rows)
                self.send(2, k, piece.at[peer], piece_in.at[k], (peer, self.me_col))
        elif number == 3:
            total = piece[me_row]
            for k in range(1, rows):
                total = total + piece_in[k]
            out[core, chip, me_row] = total.astype(jnp.bfloat16)
            mine = out.at[core, chip, me_row]
            for k in range(1, rows):
                self.send(3, k, mine, mine, (lax.rem(me_row + k, rows), self.me_col))
        elif number == 4:
            mine = out.at[core, chip]
            for k in range(1, chips):
                self.send(4, k, mine, mine, (me_row, lax.rem(chip + k, chips) * 2 + core))
        elif number == 5:
            self.send(5, 0, out.at[core], out.at[core], (me_row, chip * 2 + 1 - core))
        else:
            for copy in self.sent:
                copy.wait_send()


def reduce_kernel(rows, cols, src_ref, out_ref, *scratch):
    me_row, me_col = lax.axis_index("row"), lax.axis_index("col")
    place = (me_row, me_col, me_col // 2, lax.rem(me_col, 2))
    bufs, flat = scratch[:5], scratch[5:]
    sems = [(flat[2 * i], flat[2 * i + 1]) for i in range(6)]
    enter(rows, cols, me_row, me_col)
    count = src_ref.shape[0]
    segments = [
        Segment(rows, cols, s, place, src_ref, out_ref, bufs, sems) for s in range(count)
    ]
    for number in range(2):
        for segment in segments:
            segment.step(number)
    for time in range(4 + count):
        for s in range(count):
            if 0 <= time - s < 4:
                segments[s].step(2 + time - s)
    for segment in segments:
        segment.step(6)


def reduce_everywhere(rows, cols, stacked):
    chips = cols // 2
    unit = 16 * 2 * chips * rows
    segments = 6 if stacked.shape[0] % (6 * unit) == 0 else 3
    depth = stacked.shape[0] // (segments * 2 * chips * rows)
    shape = (segments, 2, chips, rows, depth, WIDTH)
    vmem = pl.BlockSpec(memory_space=pltpu.VMEM)
    dma = pltpu.SemaphoreType.DMA
    peers = [1, chips, rows, rows, chips, 1]
    out = pl.pallas_call(
        functools.partial(reduce_kernel, rows, cols),
        out_shape=jax.ShapeDtypeStruct(shape, jnp.bfloat16),
        in_specs=[vmem],
        out_specs=vmem,
        scratch_shapes=[
            pltpu.VMEM((segments, chips, rows, depth, WIDTH), jnp.float32),
            pltpu.VMEM((segments, chips, rows, depth, WIDTH), jnp.bfloat16),
            pltpu.VMEM((segments, chips, rows, depth, WIDTH), jnp.bfloat16),
            pltpu.VMEM((segments, rows, depth, WIDTH), jnp.float32),
            pltpu.VMEM((segments, rows, depth, WIDTH), jnp.float32),
        ]
        + [dma((segments, count)) for count in peers for _ in range(2)],
        compiler_params=pltpu.CompilerParams(
            collective_id=1, has_side_effects=True, vmem_limit_bytes=48 * 2**20
        ),
    )(stacked.reshape(shape))
    return out.reshape(stacked.shape)


def unstack_kernel(stacked_ref, *out_refs):
    start = 0
    for out in out_refs:
        height = out.shape[0]
        for c in range(out.shape[1] // WIDTH):
            for i in range(0, height, 256):
                piece = stacked_ref[start + i : start + i + 256, :].astype(jnp.float32)
                out[i : i + 256, c * WIDTH : (c + 1) * WIDTH] = piece
            start += height


def unstack(stacked, shapes):
    vmem = pl.BlockSpec(memory_space=pltpu.VMEM)
    return pl.pallas_call(
        unstack_kernel,
        out_shape=tuple(jax.ShapeDtypeStruct(shape, jnp.float32) for shape in shapes),
        in_specs=[vmem],
        out_specs=(vmem,) * len(shapes),
        compiler_params=pltpu.CompilerParams(vmem_limit_bytes=24 * 2**20),
    )(stacked)


VFRAMES = 64


def dot(left, right, dims):
    return lax.dot_general(left, right, (dims, ((), ())), preferred_element_type=jnp.float32)


AB = ((1,), (0,))
ABT = ((1,), (1,))
ATB = ((0,), (0,))


def earlier(values):
    row = lax.broadcasted_iota(jnp.int32, values.shape, 0)
    return jnp.where(lax.rem(row, VFRAMES) == 0, 0.0, pltpu.roll(values, 1, 0))


def later(values):
    row = lax.broadcasted_iota(jnp.int32, values.shape, 0)
    return jnp.where(
        lax.rem(row, VFRAMES) == VFRAMES - 1, 0.0, pltpu.roll(values, values.shape[0] - 1, 0)
    )


def logistic(values):
    return 1.0 / (1.0 + jnp.exp(-values))


def silu_slope(values):
    gate = logistic(values)
    return gate * (1.0 + values * (1.0 - gate))


def train_kernel(
    total_windows, id_ref, raw_ref, stats_ref, w1_ref, w2_ref, w3_ref, w4_ref, out_ref,
    plain, xb, db, pre, hat0, hat1, ab, enc2, bb, dec0, dec1, d0, d1, eb, fb, g0, g1,
):
    windows, frames, bins = raw_ref.shape
    rows = windows * VFRAMES
    ch = WIDTH
    block = min(rows, 256)
    per_chunk = stats_ref.shape[1] // 2
    count = WIN_SENSOR * frames
    bf = jnp.bfloat16

    def each_block(body):
        def run(i, carry):
            body(pl.ds(pl.multiple_of(i * block, block), block))
            return carry

        lax.fori_loop(0, rows // block, run, 0)

    def normalize(w, carry):
        sensor = id_ref[w]
        chunk, inner = sensor // per_chunk, lax.rem(sensor, per_chunk)
        center = stats_ref[chunk, pl.ds(inner, 1), :] / count
        square = stats_ref[chunk, pl.ds(per_chunk + inner, 1), :] / count
        factor = lax.rsqrt(square - center * center + EPS)
        for i in range(4):
            part = pl.ds(i * (frames // 4), frames // 4)
            value = (jnp.log(1.0 + raw_ref[w, part, :].astype(jnp.float32)) - center) * factor
            for c in range(4):
                plain[c, part, :] = value[:, c * 128 : (c + 1) * 128]
        at = pl.ds(pl.multiple_of(w * VFRAMES, VFRAMES), VFRAMES)
        for c in range(4):
            quarter = [plain[c, pl.ds(p, VFRAMES, stride=4), :] for p in range(4)]
            six = [earlier(quarter[3])] + quarter + [later(quarter[0])]
            for p in range(6):
                start = p * bins + c * 128
                xb[at, start : start + 128] = six[p].astype(bf)
        return carry

    lax.fori_loop(0, windows, normalize, 0)

    def first_layer(at):
        for q in range(2):
            pre[q, at, :] = dot(xb[at, 1024 * q : 1024 * q + 2048], w1_ref[...], AB)

    each_block(first_layer)
    mean = jnp.sum(pre[0] + pre[1], axis=0, keepdims=True) / (2 * rows)
    spread = jnp.square(pre[0] - mean) + jnp.square(pre[1] - mean)
    inverse = lax.rsqrt(jnp.sum(spread, axis=0, keepdims=True) / (2 * rows) + EPS)

    def forward(at):
        h0 = (pre[0, at, :] - mean) * inverse
        h1 = (pre[1, at, :] - mean) * inverse
        hat0[at, :] = h0
        hat1[at, :] = h1
        a0, a1 = h0 * logistic(h0), h1 * logistic(h1)
        for i, value in enumerate((earlier(a1), a0, a1, later(a0))):
            ab[at, i * ch : (i + 1) * ch] = value.astype(bf)
        e = dot(ab[at, :], w2_ref[...], AB)
        enc2[at, :] = e
        low = (e * logistic(e)).astype(bf)
        bb[at, :] = low
        z = [dot(low, w3_ref[:, i * ch : (i + 1) * ch], AB) for i in range(4)]
        p0, p1 = z[1] + earlier(z[3]), z[2] + later(z[0])
        dec0[at, :] = p0
        dec1[at, :] = p1
        o0, o1 = (p0 * logistic(p0)).astype(bf), (p1 * logistic(p1)).astype(bf)
        d0[at, :] = o0
        d1[at, :] = o1
        for c in range(bins // 256):
            def y(value, i):
                start = i * bins + c * 256
                return dot(value, w4_ref[:, start : start + 256], AB)

            rebuilt = (
                y(o0, 1) + earlier(y(o1, 3)),
                y(o0, 2) + y(o1, 0),
                y(o1, 1) + y(o0, 3),
                y(o1, 2) + later(y(o0, 0)),
            )
            delta = []
            for p in range(4):
                start = (p + 1) * bins + c * 256
                normed = xb[at, start : start + 256].astype(jnp.float32)
                delta.append((rebuilt[p] - normed) / total_windows)
            six = [earlier(delta[3])] + delta + [later(delta[0])]
            for p in range(6):
                start = p * bins + c * 256
                db[at, start : start + 256] = six[p].astype(bf)

    each_block(forward)

    def grad_dec2(i, carry):
        left = pl.ds(pl.multiple_of(i * ch, ch), ch)
        right = pl.ds(pl.multiple_of(2 * bins + i * ch, ch), ch)
        out_ref[left, :] = dot(d0[...], db[:, left], ATB) + dot(d1[...], db[:, right], ATB)
        return carry

    lax.fori_loop(0, 4 * bins // ch, grad_dec2, 0)

    def backward(at):
        e0 = dot(db[at, 0:2048], w4_ref[...], ABT) * silu_slope(dec0[at, :])
        e1 = dot(db[at, 1024:3072], w4_ref[...], ABT) * silu_slope(dec1[at, :])
        for i, value in enumerate((earlier(e1), e0, e1, later(e0))):
            eb[at, i * ch : (i + 1) * ch] = value.astype(bf)
        f = (dot(eb[at, :], w3_ref[...], ABT) * silu_slope(enc2[at, :])).astype(bf)
        fb[at, :] = f
        z = [dot(f, w2_ref[i * ch : (i + 1) * ch, :], ABT) for i in range(4)]
        pre[0, at, :] = (z[1] + earlier(z[3])) * silu_slope(hat0[at, :])
        pre[1, at, :] = (z[2] + later(z[0])) * silu_slope(hat1[at, :])

    each_block(backward)
    base = 4 * bins
    for i in range(4):
        out_ref[base + i * ch : base + (i + 1) * ch, :] = dot(bb[...], eb[:, i * ch : (i + 1) * ch], ATB)
    base += 4 * ch
    for i in range(4):
        out_ref[base + i * ch : base + (i + 1) * ch, :] = dot(ab[:, i * ch : (i + 1) * ch], fb[...], ATB)
    base += 4 * ch
    first = jnp.sum(pre[0] + pre[1], axis=0, keepdims=True) / (2 * rows)
    second = jnp.sum(pre[0] * hat0[...] + pre[1] * hat1[...], axis=0, keepdims=True) / (2 * rows)

    def last(at):
        g0[at, :] = ((pre[0, at, :] - first - hat0[at, :] * second) * inverse).astype(bf)
        g1[at, :] = ((pre[1, at, :] - first - hat1[at, :] * second) * inverse).astype(bf)

    each_block(last)

    def grad_enc1(i, carry):
        left = pl.ds(pl.multiple_of(i * ch, ch), ch)
        right = pl.ds(pl.multiple_of(2 * bins + i * ch, ch), ch)
        to = pl.ds(pl.multiple_of(base + i * ch, ch), ch)
        out_ref[to, :] = dot(xb[:, left], g0[...], ATB) + dot(xb[:, right], g1[...], ATB)
        return carry

    lax.fori_loop(0, 4 * bins // ch, grad_enc1, 0)


def train(total_windows, ids, raw, stats, w_enc1, w_enc2, w_dec1, w_dec2):
    windows, frames, bins = raw.shape
    rows = windows * VFRAMES
    vmem = pl.BlockSpec(memory_space=pltpu.VMEM)

    def wide(columns):
        return pltpu.VMEM((rows, columns), jnp.bfloat16)

    def full(columns):
        return pltpu.VMEM((rows, columns), jnp.float32)

    return pl.pallas_call(
        functools.partial(train_kernel, total_windows),
        out_shape=jax.ShapeDtypeStruct((8 * bins + 8 * WIDTH, WIDTH), jnp.float32),
        in_specs=[pl.BlockSpec(memory_space=pltpu.SMEM)] + [vmem] * 6,
        out_specs=vmem,
        scratch_shapes=[
            pltpu.VMEM((4, frames, 128), jnp.float32),
            wide(6 * bins),
            wide(6 * bins),
            pltpu.VMEM((2, rows, WIDTH), jnp.float32),
            full(WIDTH), full(WIDTH),
            wide(4 * WIDTH),
            full(WIDTH),
            wide(WIDTH),
            full(WIDTH), full(WIDTH),
            wide(WIDTH), wide(WIDTH),
            wide(4 * WIDTH),
            wide(WIDTH), wide(WIDTH), wide(WIDTH),
        ],
        compiler_params=pltpu.CompilerParams(vmem_limit_bytes=(40 if windows <= 8 else 56) * 2**20),
    )(ids, raw, stats, w_enc1, w_enc2, w_dec1, w_dec2)


def sensor_table(sensor_col, sensor_total):
    return (sensor_col[:, None] == jnp.arange(sensor_total, dtype=jnp.int32)[None, :]).astype(
        jnp.float32
    )


def local(spectra, sensor_ids, permutation, w_enc1, w_enc2, w_dec1, w_dec2):
    window_count = spectra.shape[0]
    frame_count = spectra.shape[1]
    row_count = lax.axis_size("row")
    col_count = lax.axis_size("col")
    total_windows = window_count * row_count * col_count
    sensor_total = total_windows // WIN_SENSOR
    per_row = col_count // row_count
    sensor_col = sensor_ids[:, 0]
    trainer = permutation // window_count
    target = trainer // col_count * per_row + trainer % per_row
    slots = jnp.arange(window_count, dtype=jnp.int32)
    order = jnp.sum(jnp.where(target[None, :] == slots[:, None], slots[None, :], 0), axis=1)
    owner = jnp.sum(
        jnp.where(target[None, :] == slots[:, None], sensor_col[None, :], 0), axis=1
    )
    per_chunk = sensor_total // col_count
    table = sensor_table(owner, sensor_total).T.reshape(col_count, per_chunk, window_count)
    blank = jnp.zeros_like(table)
    table = jnp.concatenate(
        [
            jnp.concatenate([table, blank], axis=2),
            jnp.concatenate([blank, table], axis=2),
        ],
        axis=1,
    )
    labels = jnp.broadcast_to(owner[:, None, None], (window_count, 8, 128))
    raw, labels, stats = exchange(row_count, col_count, order, spectra, labels, table)
    stacked = train(
        total_windows, labels[:, 0, 0], raw, stats, w_enc1, w_enc2, w_dec1, w_dec2
    )
    stacked = reduce_everywhere(row_count, col_count, stacked)
    grads = unstack(stacked, [w.shape for w in (w_dec2, w_dec1, w_enc2, w_enc1)])
    return tuple(grads[::-1])


def solution(mesh):
    return jax.shard_map(
        local,
        mesh=mesh,
        in_specs=(
            P(("row", "col"), None, None),
            P(("row", "col"), None),
            P(("row", "col")),
            P(),
            P(),
            P(),
            P(),
        ),
        out_specs=(P(), P(), P(), P()),
        check_vma=False,
    )
```

```python
import functools

import jax
import jax.numpy as jnp
from jax import lax
from jax.experimental import pallas as pl
from jax.experimental.pallas import tpu as pltpu
from jax.sharding import PartitionSpec as P

WIN_SENSOR = 8


EPS = 1e-05
MESH = pl.DeviceIdType.MESH
WIDTH = 256


def enter(rows, cols, me_row, me_col):
    barrier = pltpu.get_barrier_semaphore()
    for k in range(1, cols):
        pl.semaphore_signal(
            barrier, inc=1, device_id=(me_row, lax.rem(me_col + k, cols)), device_id_type=MESH
        )
    for k in range(1, rows):
        pl.semaphore_signal(
            barrier, inc=1, device_id=(lax.rem(me_row + k, rows), me_col), device_id_type=MESH
        )
    pl.semaphore_wait(barrier, rows + cols - 2)


def send(src, dst, send_sem, recv_sem, device):
    copy = pltpu.make_async_remote_copy(
        src_ref=src,
        dst_ref=dst,
        send_sem=send_sem,
        recv_sem=recv_sem,
        device_id=device,
        device_id_type=MESH,
    )
    copy.start()
    return copy


def exchange_kernel(
    rows, cols, order_ref, spectra_ref, label_ref, table_ref,
    raw_ref, got_label_ref, stats_ref,
    sorted_buf, sums, part, part_in, share, share_in,
    raw_send, raw_recv, lab_send, lab_recv, a_send, a_recv, b_send, b_recv, c_send, c_recv,
):
    me_row, me_col = lax.axis_index("row"), lax.axis_index("col")
    windows, frames, _ = spectra_ref.shape
    step = 64
    for w in range(windows):
        sorted_buf[w] = spectra_ref[order_ref[w]]
    enter(rows, cols, me_row, me_col)
    copies = []

    def batch(number, start, size):
        part = pl.ds(start, size)
        for k in range(1, cols):
            peer = lax.rem(me_col + k, cols)
            copies.append(
                send(
                    sorted_buf.at[peer, part], raw_ref.at[me_col, part],
                    raw_send.at[number, k], raw_recv.at[number, k], (me_row, peer),
                )
            )

    batch(0, 0, frames // 2)
    for k in range(1, cols):
        peer = lax.rem(me_col + k, cols)
        device = (me_row, peer)
        copies.append(send(label_ref.at[peer], got_label_ref.at[me_col], lab_send.at[k], lab_recv.at[k], device))
    raw_ref[me_col] = sorted_buf[me_col]
    got_label_ref[me_col] = label_ref[me_col]

    def window_sums(w, carry):
        def chunk(i, acc):
            total, square = acc
            values = jnp.log(1.0 + sorted_buf[w, pl.ds(pl.multiple_of(i * step, step), step), :].astype(jnp.float32))
            values = values.reshape(step // 8, 8, values.shape[1])
            return total + jnp.sum(values, axis=0), square + jnp.sum(values * values, axis=0)

        blank = jnp.zeros((8, spectra_ref.shape[2]), jnp.float32)
        total, square = lax.fori_loop(0, frames // step, chunk, (blank, blank))
        sums[w] = jnp.sum(total, axis=0, keepdims=True)
        sums[windows + w] = jnp.sum(square, axis=0, keepdims=True)
        return carry

    lax.fori_loop(0, windows, window_sums, 0)

    def spread(c, carry):
        total = jnp.zeros(part.shape[1:], jnp.float32)
        for w in range(2 * windows):
            total = total + table_ref[c, :, w : w + 1] * sums[w]
        part[c] = total
        return carry

    lax.fori_loop(0, cols, spread, 0)

    first = []
    for k in range(1, cols):
        peer = lax.rem(me_col + k, cols)
        first.append(send(part.at[peer], part_in.at[k], a_send.at[k], a_recv.at[k], (me_row, peer)))
    batch(1, frames // 2, frames * 3 // 8)
    total = part[me_col]
    for k in range(1, cols):
        first[k - 1].wait_recv()
        total = total + part_in[k]
    share[...] = total
    second = []
    for k in range(1, rows):
        peer = lax.rem(me_row + k, rows)
        second.append(send(share, share_in.at[me_row], b_send.at[k], b_recv.at[k], (peer, me_col)))
    share_in[me_row] = total
    for copy in second:
        copy.wait_recv()
    total = share_in[0]
    for r in range(1, rows):
        total = total + share_in[r]
    stats_ref[me_col] = total
    third = []
    for k in range(1, cols):
        peer = lax.rem(me_col + k, cols)
        third.append(send(stats_ref.at[me_col], stats_ref.at[me_col], c_send.at[k], c_recv.at[k], (me_row, peer)))
    batch(2, frames * 7 // 8, frames // 8)
    for copy in third + copies:
        copy.wait_recv()
    for copy in first + second + third + copies:
        copy.wait_send()


def exchange(rows, cols, order, spectra, labels, table):
    windows, frames, bins = spectra.shape
    depth = table.shape[1]
    vmem = pl.BlockSpec(memory_space=pltpu.VMEM)
    dma = pltpu.SemaphoreType.DMA
    return pl.pallas_call(
        functools.partial(exchange_kernel, rows, cols),
        out_shape=(
            jax.ShapeDtypeStruct((cols, frames, bins), jnp.bfloat16),
            jax.ShapeDtypeStruct(labels.shape, jnp.int32),
            jax.ShapeDtypeStruct((cols, depth, bins), jnp.float32),
        ),
        in_specs=[pl.BlockSpec(memory_space=pltpu.SMEM), vmem, vmem, vmem],
        out_specs=(vmem, vmem, vmem),
        scratch_shapes=[
            pltpu.VMEM((windows, frames, bins), jnp.bfloat16),
            pltpu.VMEM((2 * windows, 1, bins), jnp.float32),
            pltpu.VMEM((cols, depth, bins), jnp.float32),
            pltpu.VMEM((cols, depth, bins), jnp.float32),
            pltpu.VMEM((depth, bins), jnp.float32),
            pltpu.VMEM((rows, depth, bins), jnp.float32),
        ]
        + [dma((3, cols))] * 2 + [dma((cols,))] * 4 + [dma((rows,))] * 2 + [dma((cols,))] * 2,
        compiler_params=pltpu.CompilerParams(
            collective_id=0, has_side_effects=True, vmem_limit_bytes=48 * 2**20
        ),
    )(order, spectra, labels, table)


class Segment:
    def __init__(self, rows, cols, index, place, src, out, bufs, sems):
        self.rows, self.chips, self.index = rows, cols // 2, index
        self.me_row, self.me_col, self.chip, self.core = place
        self.src, self.out, self.bufs, self.sems = src, out, bufs, sems
        self.open, self.sent = [], []

    def send(self, step, k, src, dst, device):
        send_sem, recv_sem = self.sems[step]
        copy = send(src, dst, send_sem.at[self.index, k], recv_sem.at[self.index, k], device)
        self.open.append(copy)
        self.sent.append(copy)

    def land(self):
        for copy in self.open:
            copy.wait_recv()
        self.open = []

    def step(self, number):
        half_in, quarter, quarter_in, piece, piece_in = (b.at[self.index] for b in self.bufs)
        out, chips, rows = self.out.at[self.index], self.chips, self.rows
        core, chip, me_row = self.core, self.chip, self.me_row
        self.land()
        if number == 0:
            other = 1 - core
            self.send(0, 0, self.src.at[self.index, other], half_in, (me_row, chip * 2 + other))
        elif number == 1:
            def add(q, carry):
                quarter[q] = (self.src[self.index, core, q] + half_in[q]).astype(jnp.bfloat16)
                return carry

            lax.fori_loop(0, chips, add, 0)
            for k in range(1, chips):
                peer = lax.rem(chip + k, chips)
                self.send(1, k, quarter.at[peer], quarter_in.at[k], (me_row, peer * 2 + core))
        elif number == 2:
            def add(r, carry):
                total = self.src[self.index, core, chip, r] + half_in[chip, r]
                for k in range(1, chips):
                    total = total + quarter_in[k, r].astype(jnp.float32)
                piece[r] = total
                return carry

            lax.fori_loop(0, rows, add, 0)
            for k in range(1, rows):
                peer = lax.rem(me_row + k, rows)
                self.send(2, k, piece.at[peer], piece_in.at[k], (peer, self.me_col))
        elif number == 3:
            total = piece[me_row]
            for k in range(1, rows):
                total = total + piece_in[k]
            out[core, chip, me_row] = total.astype(jnp.bfloat16)
            mine = out.at[core, chip, me_row]
            for k in range(1, rows):
                self.send(3, k, mine, mine, (lax.rem(me_row + k, rows), self.me_col))
        elif number == 4:
            mine = out.at[core, chip]
            for k in range(1, chips):
                self.send(4, k, mine, mine, (me_row, lax.rem(chip + k, chips) * 2 + core))
        elif number == 5:
            self.send(5, 0, out.at[core], out.at[core], (me_row, chip * 2 + 1 - core))
        else:
            for copy in self.sent:
                copy.wait_send()


def reduce_kernel(rows, cols, src_ref, out_ref, *scratch):
    me_row, me_col = lax.axis_index("row"), lax.axis_index("col")
    place = (me_row, me_col, me_col // 2, lax.rem(me_col, 2))
    bufs, flat = scratch[:5], scratch[5:]
    sems = [(flat[2 * i], flat[2 * i + 1]) for i in range(6)]
    enter(rows, cols, me_row, me_col)
    count = src_ref.shape[0]
    segments = [
        Segment(rows, cols, s, place, src_ref, out_ref, bufs, sems) for s in range(count)
    ]
    for number in range(2):
        for segment in segments:
            segment.step(number)
    for time in range(4 + count):
        for s in range(count):
            if 0 <= time - s < 4:
                segments[s].step(2 + time - s)
    for segment in segments:
        segment.step(6)


def reduce_everywhere(rows, cols, stacked):
    chips = cols // 2
    unit = 16 * 2 * chips * rows
    segments = 6 if stacked.shape[0] % (6 * unit) == 0 else 3
    depth = stacked.shape[0] // (segments * 2 * chips * rows)
    shape = (segments, 2, chips, rows, depth, WIDTH)
    vmem = pl.BlockSpec(memory_space=pltpu.VMEM)
    dma = pltpu.SemaphoreType.DMA
    peers = [1, chips, rows, rows, chips, 1]
    out = pl.pallas_call(
        functools.partial(reduce_kernel, rows, cols),
        out_shape=jax.ShapeDtypeStruct(shape, jnp.bfloat16),
        in_specs=[vmem],
        out_specs=vmem,
        scratch_shapes=[
            pltpu.VMEM((segments, chips, rows, depth, WIDTH), jnp.float32),
            pltpu.VMEM((segments, chips, rows, depth, WIDTH), jnp.bfloat16),
            pltpu.VMEM((segments, chips, rows, depth, WIDTH), jnp.bfloat16),
            pltpu.VMEM((segments, rows, depth, WIDTH), jnp.float32),
            pltpu.VMEM((segments, rows, depth, WIDTH), jnp.float32),
        ]
        + [dma((segments, count)) for count in peers for _ in range(2)],
        compiler_params=pltpu.CompilerParams(
            collective_id=1, has_side_effects=True, vmem_limit_bytes=48 * 2**20
        ),
    )(stacked.reshape(shape))
    return out.reshape(stacked.shape)


def unstack_kernel(stacked_ref, *out_refs):
    start = 0
    for out in out_refs:
        height = out.shape[0]
        for c in range(out.shape[1] // WIDTH):
            for i in range(0, height, 256):
                piece = stacked_ref[start + i : start + i + 256, :].astype(jnp.float32)
                out[i : i + 256, c * WIDTH : (c + 1) * WIDTH] = piece
            start += height


def unstack(stacked, shapes):
    vmem = pl.BlockSpec(memory_space=pltpu.VMEM)
    return pl.pallas_call(
        unstack_kernel,
        out_shape=tuple(jax.ShapeDtypeStruct(shape, jnp.float32) for shape in shapes),
        in_specs=[vmem],
        out_specs=(vmem,) * len(shapes),
        compiler_params=pltpu.CompilerParams(vmem_limit_bytes=24 * 2**20),
    )(stacked)


VFRAMES = 64


def dot(left, right, dims):
    return lax.dot_general(left, right, (dims, ((), ())), preferred_element_type=jnp.float32)


AB = ((1,), (0,))
ABT = ((1,), (1,))
ATB = ((0,), (0,))


def earlier(values):
    row = lax.broadcasted_iota(jnp.int32, values.shape, 0)
    return jnp.where(lax.rem(row, VFRAMES) == 0, 0.0, pltpu.roll(values, 1, 0))


def later(values):
    row = lax.broadcasted_iota(jnp.int32, values.shape, 0)
    return jnp.where(
        lax.rem(row, VFRAMES) == VFRAMES - 1, 0.0, pltpu.roll(values, values.shape[0] - 1, 0)
    )


def logistic(values):
    return 1.0 / (1.0 + jnp.exp(-values))


def silu_slope(values):
    gate = logistic(values)
    return gate * (1.0 + values * (1.0 - gate))


def train_kernel(
    total_windows, id_ref, raw_ref, stats_ref, w1_ref, w2_ref, w3_ref, w4_ref, out_ref,
    plain, xb, db, pre, hat0, hat1, ab, enc2, bb, dec0, dec1, d0, d1, eb, fb, g0, g1,
):
    windows, frames, bins = raw_ref.shape
    rows = windows * VFRAMES
    ch = WIDTH
    block = min(rows, 256)
    per_chunk = stats_ref.shape[1] // 2
    count = WIN_SENSOR * frames
    bf = jnp.bfloat16

    def each_block(body):
        def run(i, carry):
            body(pl.ds(pl.multiple_of(i * block, block), block))
            return carry

        lax.fori_loop(0, rows // block, run, 0)

    def normalize(w, carry):
        sensor = id_ref[w]
        chunk, inner = sensor // per_chunk, lax.rem(sensor, per_chunk)
        center = stats_ref[chunk, pl.ds(inner, 1), :] / count
        square = stats_ref[chunk, pl.ds(per_chunk + inner, 1), :] / count
        factor = lax.rsqrt(square - center * center + EPS)
        for i in range(4):
            part = pl.ds(i * (frames // 4), frames // 4)
            value = (jnp.log(1.0 + raw_ref[w, part, :].astype(jnp.float32)) - center) * factor
            for c in range(4):
                plain[c, part, :] = value[:, c * 128 : (c + 1) * 128]
        at = pl.ds(pl.multiple_of(w * VFRAMES, VFRAMES), VFRAMES)
        for c in range(4):
            quarter = [plain[c, pl.ds(p, VFRAMES, stride=4), :] for p in range(4)]
            six = [earlier(quarter[3])] + quarter + [later(quarter[0])]
            for p in range(6):
                start = p * bins + c * 128
                xb[at, start : start + 128] = six[p].astype(bf)
        return carry

    lax.fori_loop(0, windows, normalize, 0)

    def first_layer(at):
        for q in range(2):
            pre[q, at, :] = dot(xb[at, 1024 * q : 1024 * q + 2048], w1_ref[...], AB)

    each_block(first_layer)
    mean = jnp.sum(pre[0] + pre[1], axis=0, keepdims=True) / (2 * rows)
    spread = jnp.square(pre[0] - mean) + jnp.square(pre[1] - mean)
    inverse = lax.rsqrt(jnp.sum(spread, axis=0, keepdims=True) / (2 * rows) + EPS)

    def forward(at):
        h0 = (pre[0, at, :] - mean) * inverse
        h1 = (pre[1, at, :] - mean) * inverse
        hat0[at, :] = h0
        hat1[at, :] = h1
        a0, a1 = h0 * logistic(h0), h1 * logistic(h1)
        for i, value in enumerate((earlier(a1), a0, a1, later(a0))):
            ab[at, i * ch : (i + 1) * ch] = value.astype(bf)
        e = dot(ab[at, :], w2_ref[...], AB)
        enc2[at, :] = e
        low = (e * logistic(e)).astype(bf)
        bb[at, :] = low
        z = [dot(low, w3_ref[:, i * ch : (i + 1) * ch], AB) for i in range(4)]
        p0, p1 = z[1] + earlier(z[3]), z[2] + later(z[0])
        dec0[at, :] = p0
        dec1[at, :] = p1
        o0, o1 = (p0 * logistic(p0)).astype(bf), (p1 * logistic(p1)).astype(bf)
        d0[at, :] = o0
        d1[at, :] = o1
        for c in range(bins // 256):
            def y(value, i):
                start = i * bins + c * 256
                return dot(value, w4_ref[:, start : start + 256], AB)

            rebuilt = (
                y(o0, 1) + earlier(y(o1, 3)),
                y(o0, 2) + y(o1, 0),
                y(o1, 1) + y(o0, 3),
                y(o1, 2) + later(y(o0, 0)),
            )
            delta = []
            for p in range(4):
                start = (p + 1) * bins + c * 256
                normed = xb[at, start : start + 256].astype(jnp.float32)
                delta.append((rebuilt[p] - normed) / total_windows)
            six = [earlier(delta[3])] + delta + [later(delta[0])]
            for p in range(6):
                start = p * bins + c * 256
                db[at, start : start + 256] = six[p].astype(bf)

    each_block(forward)

    def grad_dec2(i, carry):
        left = pl.ds(pl.multiple_of(i * ch, ch), ch)
        right = pl.ds(pl.multiple_of(2 * bins + i * ch, ch), ch)
        out_ref[left, :] = dot(d0[...], db[:, left], ATB) + dot(d1[...], db[:, right], ATB)
        return carry

    lax.fori_loop(0, 4 * bins // ch, grad_dec2, 0)

    def backward(at):
        e0 = dot(db[at, 0:2048], w4_ref[...], ABT) * silu_slope(dec0[at, :])
        e1 = dot(db[at, 1024:3072], w4_ref[...], ABT) * silu_slope(dec1[at, :])
        for i, value in enumerate((earlier(e1), e0, e1, later(e0))):
            eb[at, i * ch : (i + 1) * ch] = value.astype(bf)
        f = (dot(eb[at, :], w3_ref[...], ABT) * silu_slope(enc2[at, :])).astype(bf)
        fb[at, :] = f
        z = [dot(f, w2_ref[i * ch : (i + 1) * ch, :], ABT) for i in range(4)]
        pre[0, at, :] = (z[1] + earlier(z[3])) * silu_slope(hat0[at, :])
        pre[1, at, :] = (z[2] + later(z[0])) * silu_slope(hat1[at, :])

    each_block(backward)
    base = 4 * bins
    for i in range(4):
        out_ref[base + i * ch : base + (i + 1) * ch, :] = dot(bb[...], eb[:, i * ch : (i + 1) * ch], ATB)
    base += 4 * ch
    for i in range(4):
        out_ref[base + i * ch : base + (i + 1) * ch, :] = dot(ab[:, i * ch : (i + 1) * ch], fb[...], ATB)
    base += 4 * ch
    first = jnp.sum(pre[0] + pre[1], axis=0, keepdims=True) / (2 * rows)
    second = jnp.sum(pre[0] * hat0[...] + pre[1] * hat1[...], axis=0, keepdims=True) / (2 * rows)

    def last(at):
        g0[at, :] = ((pre[0, at, :] - first - hat0[at, :] * second) * inverse).astype(bf)
        g1[at, :] = ((pre[1, at, :] - first - hat1[at, :] * second) * inverse).astype(bf)

    each_block(last)

    def grad_enc1(i, carry):
        left = pl.ds(pl.multiple_of(i * ch, ch), ch)
        right = pl.ds(pl.multiple_of(2 * bins + i * ch, ch), ch)
        to = pl.ds(pl.multiple_of(base + i * ch, ch), ch)
        out_ref[to, :] = dot(xb[:, left], g0[...], ATB) + dot(xb[:, right], g1[...], ATB)
        return carry

    lax.fori_loop(0, 4 * bins // ch, grad_enc1, 0)


def train(total_windows, ids, raw, stats, w_enc1, w_enc2, w_dec1, w_dec2):
    windows, frames, bins = raw.shape
    rows = windows * VFRAMES
    vmem = pl.BlockSpec(memory_space=pltpu.VMEM)

    def wide(columns):
        return pltpu.VMEM((rows, columns), jnp.bfloat16)

    def full(columns):
        return pltpu.VMEM((rows, columns), jnp.float32)

    return pl.pallas_call(
        functools.partial(train_kernel, total_windows),
        out_shape=jax.ShapeDtypeStruct((8 * bins + 8 * WIDTH, WIDTH), jnp.float32),
        in_specs=[pl.BlockSpec(memory_space=pltpu.SMEM)] + [vmem] * 6,
        out_specs=vmem,
        scratch_shapes=[
            pltpu.VMEM((4, frames, 128), jnp.float32),
            wide(6 * bins),
            wide(6 * bins),
            pltpu.VMEM((2, rows, WIDTH), jnp.float32),
            full(WIDTH), full(WIDTH),
            wide(4 * WIDTH),
            full(WIDTH),
            wide(WIDTH),
            full(WIDTH), full(WIDTH),
            wide(WIDTH), wide(WIDTH),
            wide(4 * WIDTH),
            wide(WIDTH), wide(WIDTH), wide(WIDTH),
        ],
        compiler_params=pltpu.CompilerParams(vmem_limit_bytes=(40 if windows <= 8 else 56) * 2**20),
    )(ids, raw, stats, w_enc1, w_enc2, w_dec1, w_dec2)


def sensor_table(sensor_col, sensor_total):
    return (sensor_col[:, None] == jnp.arange(sensor_total, dtype=jnp.int32)[None, :]).astype(
        jnp.float32
    )


def local(spectra, sensor_ids, permutation, w_enc1, w_enc2, w_dec1, w_dec2):
    window_count = spectra.shape[0]
    frame_count = spectra.shape[1]
    row_count = lax.axis_size("row")
    col_count = lax.axis_size("col")
    total_windows = window_count * row_count * col_count
    sensor_total = total_windows // WIN_SENSOR
    per_row = col_count // row_count
    sensor_col = sensor_ids[:, 0]
    trainer = permutation // window_count
    target = trainer // col_count * per_row + trainer % per_row
    slots = jnp.arange(window_count, dtype=jnp.int32)
    order = jnp.sum(jnp.where(target[None, :] == slots[:, None], slots[None, :], 0), axis=1)
    owner = jnp.sum(
        jnp.where(target[None, :] == slots[:, None], sensor_col[None, :], 0), axis=1
    )
    per_chunk = sensor_total // col_count
    table = sensor_table(owner, sensor_total).T.reshape(col_count, per_chunk, window_count)
    blank = jnp.zeros_like(table)
    table = jnp.concatenate(
        [
            jnp.concatenate([table, blank], axis=2),
            jnp.concatenate([blank, table], axis=2),
        ],
        axis=1,
    )
    labels = jnp.broadcast_to(owner[:, None, None], (window_count, 8, 128))
    raw, labels, stats = exchange(row_count, col_count, order, spectra, labels, table)
    stacked = train(
        total_windows, labels[:, 0, 0], raw, stats, w_enc1, w_enc2, w_dec1, w_dec2
    )
    stacked = reduce_everywhere(row_count, col_count, stacked)
    grads = unstack(stacked, [w.shape for w in (w_dec2, w_dec1, w_enc2, w_enc1)])
    return tuple(grads[::-1])


def solution(mesh):
    return jax.shard_map(
        local,
        mesh=mesh,
        in_specs=(
            P(("row", "col"), None, None),
            P(("row", "col"), None),
            P(("row", "col")),
            P(),
            P(),
            P(),
            P(),
        ),
        out_specs=(P(), P(), P(), P()),
        check_vma=False,
    )
```
